32 devices in a mesh: cells: 32 (over z, y, x, core).
Axes of the slice: x: 2, y: 2, z: 4, core: 2. Of those that a mesh axis runs over, the one named last changes fastest.
Arguments:
- earlier_kinetics_concentrations: float32 [4096, 1536], P('cells'), may hold values from 0.05 to 1
- thermal_level: float32 [4096], P('cells'), may hold values from 0.8 to 2
- earlier_fluid_holder: int32 [4096], P('cells'), may hold values from 0 to 31, as said below
- earlier_fluid_slot: int32 [4096], P('cells'), may hold values from 0 to 127, as said below
- adjacent_volumes: int32 [6, 4096], P(None, 'cells'), may hold values from 0 to 4095, as said below
- interface_spreading_factor: float32 [6, 4096], P(None, 'cells'), may hold values from 0.2 to 1
- species_spreading_coefficient: float32 [1536], replicated, may hold values from 0.1 to 2
- present_kinetics_holder: int32 [4096], P('cells'), may hold values from 0 to 31, as said below
- present_kinetics_slot: int32 [4096], P('cells'), may hold values from 0 to 127, as said below
- natural_frequency_factor: float32 [4608], replicated, may hold values from -0.5 to 1
- arrhenius_energy: float32 [4608], replicated, may hold values from 0 to 2
- consumed_species: int32 [2, 4608], replicated, may hold values from 0 to 1535
- yielded_species: int32 [2, 4608], replicated, may hold values from 0 to 1535
Outputs:
- spread_concentration: float32 [4096, 1536], P('cells')
- chem_next: float32 [4096, 1536], P('cells')
The draws below stay inside these ranges and needn't reach their ends.
Inputs may be any that keep to these rules, and one draw needn't show every extreme that they name: earlier_fluid_holder and earlier_fluid_slot together name every row of every flow owner exactly once; each device hands exactly 2 of its rows to each of 12 other devices and keeps the rest; each device receives exactly 2 rows from each of 12 devices. `earlier_fluid_slot`: rows of one flow owner. `adjacent_volumes`: each face names another cell at most 32 positions away in the flow order; on every device some face reaches exactly 32 away. present_kinetics_holder and present_kinetics_slot together name every row of every chemistry owner exactly once; each device hands exactly 2 of its cells to each of 12 other devices and keeps the rest; each device receives exactly 2 cells from each of 12 devices. `present_kinetics_slot`: rows of one chemistry owner.
All inputs are finite; a program needn't handle non-finite values.
Results may differ from the reference program's by a relative error of at most 0.0018.
Values sent between devices are 32-bit elements; how exact they have to be, the bound alone decides.
No kernel may reach another device: no remote copies, remote signals or barrier semaphores. Data moves between devices by JAX's collectives and lax.ppermute only.
A program may use at most 64 MiB of HBM per device.

```python
import math
import jax
import jax.numpy as jnp
from jax import lax

SPECIES = 1536
REACTIONS = 4608
ROWS = 128
NEWTON = 2
FACES = 6
HALO = 32
CAP = 2
PEERS = 12
GRID_VOLUMES_ALL = 4096
N_CELLS = 32


def routing_lists(key):
    devices = GRID_VOLUMES_ALL // ROWS
    keys = jax.random.split(key, 5)
    relabel = jax.random.permutation(keys[0], devices).astype(jnp.int32)
    position = jnp.zeros((devices,), jnp.int32).at[relabel].set(jnp.arange(devices, dtype=jnp.int32))
    shifts = (jax.random.permutation(keys[1], devices - 1)[:PEERS] + 1).astype(jnp.int32)
    counts = jnp.full((PEERS,), CAP, jnp.int32)
    bounds = jnp.cumsum(counts)
    sent_total = bounds[PEERS - 1]
    row_rank = jax.vmap(lambda sub_key: jax.random.permutation(sub_key, ROWS))(jax.random.split(keys[3], devices)).astype(jnp.int32)
    arrival = jax.vmap(lambda sub_key: jax.random.permutation(sub_key, ROWS))(jax.random.split(keys[4], devices)).astype(jnp.int32)
    device = (jnp.arange(GRID_VOLUMES_ALL, dtype=jnp.int32) // ROWS).astype(jnp.int32)
    rank = row_rank.reshape(-1)
    group = jnp.sum((rank[:, None] >= bounds[None, :]).astype(jnp.int32), axis=1)
    group = jnp.minimum(group, PEERS - 1)
    target = relabel[(position[device] + shifts[group]) % devices]
    owner = jnp.where(rank < sent_total, target, device).astype(jnp.int32)
    slot_ids = arrival[owner, rank].astype(jnp.int32)
    return (owner, slot_ids)


def draw_earlier_fluid_holder(key, part):
    return routing_lists(jax.random.fold_in(key, 11))[0]


def draw_earlier_fluid_slot(key, part):
    return routing_lists(jax.random.fold_in(key, 11))[1]


def draw_present_kinetics_holder(key, part):
    return routing_lists(jax.random.fold_in(key, 23))[0]


def draw_present_kinetics_slot(key, part):
    return routing_lists(jax.random.fold_in(key, 23))[1]


def draw_adjacent_volumes(key, part):
    keys = jax.random.split(jax.random.fold_in(key, 37), 2)
    distance = jax.random.randint(keys[0], (FACES, GRID_VOLUMES_ALL), 1, HALO + 1).astype(jnp.int32)
    sign_value = (jax.random.randint(keys[1], (FACES, GRID_VOLUMES_ALL), 0, 2) * 2 - 1).astype(jnp.int32)
    cell_index = jnp.arange(GRID_VOLUMES_ALL, dtype=jnp.int32)[None, :]
    face_index = jnp.arange(FACES, dtype=jnp.int32)[:, None]
    distance = jnp.where((face_index == 0) & (cell_index % ROWS == ROWS - 1), HALO, distance)
    forward = cell_index + sign_value * distance
    chosen = jnp.where((forward < 0) | (forward >= GRID_VOLUMES_ALL), cell_index - sign_value * distance, forward)
    return chosen.astype(jnp.int32)


def place_ends(values, rng, smallest, high):
    dims = values.shape
    spot = [jax.random.randint(jax.random.fold_in(rng, axis), (), 0, dims[axis]) for axis in range(len(dims))]
    values = values.at[tuple(spot)].set(smallest)
    longest = dims.index(max(dims))
    spot[longest] = (spot[longest] + 1) % dims[longest]
    return values.at[tuple(spot)].set(high)


def block_levels(own_key, shape, shards, low, top_value):
    gain = 1.0
    for dim, parts in shards:
        heights = jax.random.uniform(jax.random.fold_in(jax.random.fold_in(own_key, 6), dim), (parts,), jnp.float32, low / len(shards), top_value / len(shards))
        gain = gain * jnp.repeat(jnp.exp(heights), shape[dim] // parts).reshape((-1,) + (1,) * (len(shape) - 1 - dim))
    return gain


def setup_inputs(seed: int = 0) -> dict:
    streams_of = jax.random.split(jax.random.key(seed), 14)
    return {
        "earlier_kinetics_concentrations": jnp.clip(jnp.exp(math.log(1.0) - 2.9957323 * jax.random.uniform(streams_of[0], (GRID_VOLUMES_ALL, SPECIES), jnp.float32) ** block_levels(streams_of[0], (GRID_VOLUMES_ALL, SPECIES), ((0, 32),), -0.2, 0.2)), 0.05, 1.0),
        "thermal_level": jnp.clip(0.8 + 1.2 * jax.random.uniform(streams_of[1], (GRID_VOLUMES_ALL,), jnp.float32) ** block_levels(streams_of[1], (GRID_VOLUMES_ALL,), ((0, 32),), -0.2, 0.2), 0.8, 2.0),
        "earlier_fluid_holder": draw_earlier_fluid_holder(jax.random.fold_in(streams_of[13], 71), 0),
        "earlier_fluid_slot": draw_earlier_fluid_slot(jax.random.fold_in(streams_of[13], 71), 0),
        "adjacent_volumes": draw_adjacent_volumes(jax.random.fold_in(streams_of[13], 71), 0),
        "interface_spreading_factor": jnp.clip(0.2 + 0.8 * jax.random.uniform(streams_of[5], (FACES, GRID_VOLUMES_ALL), jnp.float32) ** block_levels(streams_of[5], (FACES, GRID_VOLUMES_ALL), ((1, 32),), -0.2, 0.2), 0.2, 1.0),
        "species_spreading_coefficient": jnp.clip(jnp.exp(jax.random.uniform(streams_of[6], (SPECIES,), jnp.float32, math.log(0.1), math.log(2.0))), 0.1, 2.0),
        "present_kinetics_holder": draw_present_kinetics_holder(jax.random.fold_in(streams_of[13], 71), 0),
        "present_kinetics_slot": draw_present_kinetics_slot(jax.random.fold_in(streams_of[13], 71), 0),
        "natural_frequency_factor": jnp.clip(jax.random.uniform(streams_of[9], (REACTIONS,), jnp.float32, -0.5, 1.0), -0.5, 1.0),
        "arrhenius_energy": jnp.clip(jax.random.uniform(streams_of[10], (REACTIONS,), jnp.float32, 0.0, 2.0), 0.0, 2.0),
        "consumed_species": place_ends(jax.random.randint(streams_of[11], (2, REACTIONS), 0, SPECIES), jax.random.fold_in(streams_of[11], 1), 0, SPECIES - 1).astype(jnp.int32),
        "yielded_species": place_ends(jax.random.randint(streams_of[12], (2, REACTIONS), 0, SPECIES), jax.random.fold_in(streams_of[12], 1), 0, SPECIES - 1).astype(jnp.int32),
    }


time_step = 0.5


def reference(earlier_kinetics_concentrations, thermal_level, earlier_fluid_holder, earlier_fluid_slot, adjacent_volumes, interface_spreading_factor, species_spreading_coefficient, present_kinetics_holder, present_kinetics_slot, natural_frequency_factor, arrhenius_energy, consumed_species, yielded_species):
    fluid_volume_position = (earlier_fluid_holder * ROWS + earlier_fluid_slot).astype(jnp.int32)
    flow_state = jnp.zeros((GRID_VOLUMES_ALL, SPECIES), jnp.float32).at[fluid_volume_position].set(earlier_kinetics_concentrations)
    fluid_volume_heat = jnp.zeros((GRID_VOLUMES_ALL,), jnp.float32).at[fluid_volume_position].set(thermal_level)
    coupling = jnp.zeros((GRID_VOLUMES_ALL, SPECIES), jnp.float32)
    for face_index in range(FACES):
        coupling = coupling + interface_spreading_factor[face_index][:, None] * flow_state[adjacent_volumes[face_index]]
    scale = time_step * species_spreading_coefficient[None, :]
    spread_concentration = (flow_state + scale * coupling) / (1.0 + scale * jnp.sum(interface_spreading_factor, axis=0)[:, None])
    kinetics_position = (present_kinetics_holder * ROWS + present_kinetics_slot).astype(jnp.int32)
    initial = jnp.zeros((GRID_VOLUMES_ALL, SPECIES), jnp.float32).at[kinetics_position].set(spread_concentration)
    reciprocal_mapping = jnp.zeros((GRID_VOLUMES_ALL,), jnp.float32).at[kinetics_position].set(1.0 / fluid_volume_heat)
    species_rows = lax.broadcasted_iota(jnp.int32, (SPECIES, REACTIONS), 0)
    react_table = (species_rows == consumed_species[0][None, :]).astype(jnp.bfloat16) + (species_rows == consumed_species[1][None, :]).astype(jnp.bfloat16)
    product_table = (species_rows == yielded_species[0][None, :]).astype(jnp.bfloat16) + (species_rows == yielded_species[1][None, :]).astype(jnp.bfloat16)

    def newton_block(pair):
        start_rows, inverse_rows = pair
        log_rate = natural_frequency_factor[None, :] - arrhenius_energy[None, :] * inverse_rows[:, None]
        current = start_rows
        for newton_turn in range(NEWTON):
            log_state = jnp.log(current).astype(jnp.bfloat16)
            exponent = jnp.dot(log_state, react_table, preferred_element_type=jnp.float32)
            rate_rows = jnp.exp(log_rate + exponent).astype(jnp.bfloat16)
            loss_sum = lax.dot_general(rate_rows, react_table, (((1,), (1,)), ((), ())), preferred_element_type=jnp.float32)
            gain_sum = lax.dot_general(rate_rows, product_table, (((1,), (1,)), ((), ())), preferred_element_type=jnp.float32)
            current = (start_rows + time_step * gain_sum) / (1.0 + time_step * loss_sum / current)
        return current

    result = lax.map(newton_block, (initial.reshape(N_CELLS, ROWS, SPECIES), reciprocal_mapping.reshape(N_CELLS, ROWS)))
    return spread_concentration, result.reshape(GRID_VOLUMES_ALL, SPECIES)
```

```python
import functools

import jax
import jax.numpy as jnp
from jax import lax
from jax.experimental import pallas as pl
from jax.experimental.pallas import tpu as pltpu
from jax.sharding import PartitionSpec as P

NEWTON = 2
HALO = 32
CAP = 2
EXTRA = 128

time_step = 0.5

f32 = jnp.float32
bf16 = jnp.bfloat16
i32 = jnp.int32
i16 = jnp.int16

VMEM = pl.BlockSpec(memory_space=pltpu.VMEM)
SMEM = pl.BlockSpec(memory_space=pltpu.SMEM)


def iota(shape, dim):
    return lax.broadcasted_iota(i32, shape, dim)


def column(row):
    n = row.shape[1]
    eye = iota((n, n), 0) == iota((n, n), 1)
    return jnp.sum(jnp.where(eye, row, jnp.zeros_like(row)), axis=1, keepdims=True)


def split3(x):
    hi = x.astype(bf16)
    rest = x - hi.astype(f32)
    mid = rest.astype(bf16)
    lo = (rest - mid.astype(f32)).astype(bf16)
    return hi, mid, lo


def pick(choice, rows, dims=(((1,), (0,)), ((), ()))):
    choice = choice.astype(bf16)
    out = None
    for part in split3(rows):
        term = lax.dot_general(choice, part, dims, preferred_element_type=f32)
        out = term if out is None else out + term
    return out


def send_choice(owner, me, partners):
    n = owner.shape[1]
    hits = ((iota((partners, n), 0) == owner) & (owner != me)).astype(f32)
    before = (iota((n, n), 0) < iota((n, n), 1)).astype(bf16)
    earlier = jnp.dot(hits.astype(bf16), before, preferred_element_type=f32)
    within = jnp.sum(earlier * hits, axis=0, keepdims=True).astype(i32)
    position = jnp.where(owner != me, owner * CAP + within, -1)
    return (iota((partners * CAP, n), 0) == position).astype(f32)


def pack(send_ref, rows, temper, owner, slot, me):
    partners, cap, _ = send_ref.shape
    n, species = rows.shape
    lane = iota((n, EXTRA), 1)
    beside = jnp.where(
        lane == 0, temper, jnp.where(lane == 1, column(slot.astype(f32)) + 1.0, 0.0)
    )
    choice = send_choice(owner, me, partners)
    send_ref[:, :, :species] = pick(choice, rows).reshape(partners, cap, species)
    send_ref[:, :, species:] = pick(choice, beside).reshape(partners, cap, EXTRA)


def unpack(recv_ref, rows, temper, owner, slot, me):
    partners, cap, width = recv_ref.shape
    n, species = rows.shape
    stay = ((iota((n, n), 0) == slot) & (owner == me)).astype(f32)
    got = recv_ref[...].reshape(partners * cap, width)
    place = got[:, species + 1 : species + 2].astype(i32) - 1
    land = (iota((partners * cap, n), 1) == place).astype(f32)
    to_rows = (((0,), (0,)), ((), ()))
    beside = jnp.broadcast_to(temper, (n, EXTRA))
    state = pick(stay, rows) + pick(land, got[:, :species], to_rows)
    heat = pick(stay, beside) + pick(land, got[:, species:], to_rows)
    return state, heat[:, 0:1]


def pack_kernel(me_ref, rows_ref, temper_ref, owner_ref, slot_ref, send_ref):
    pack(
        send_ref,
        rows_ref[...],
        column(temper_ref[...]),
        owner_ref[...],
        slot_ref[...],
        me_ref[0],
    )


def flow_kernel(
    me_ref, recv_ref, rows_ref, temper_ref, owner_ref, slot_ref, flow_ref, heat_ref, up_ref, down_ref
):
    state, heat = unpack(
        recv_ref,
        rows_ref[...],
        column(temper_ref[...]),
        owner_ref[...],
        slot_ref[...],
        me_ref[0],
    )
    n = state.shape[0]
    flow_ref[...] = state
    heat_ref[...] = jnp.broadcast_to(heat, heat_ref.shape)
    up_ref[...] = state[n - HALO :]
    down_ref[...] = state[:HALO]


def spread_kernel(
    me_ref,
    flow_ref,
    heat_ref,
    before_ref,
    after_ref,
    adjacent_ref,
    factor_ref,
    coefficient_ref,
    owner_ref,
    slot_ref,
    spread_ref,
    send_ref,
):
    me = me_ref[0]
    flow = flow_ref[...]
    n = flow.shape[0]
    faces = adjacent_ref.shape[0]
    index = adjacent_ref[...] - me * n + HALO
    factor = factor_ref[...]
    rows = iota((n + 2 * HALO, n), 0)
    weight = jnp.zeros((n + 2 * HALO, n), f32)
    total = jnp.zeros((1, n), f32)
    for face in range(faces):
        weight += jnp.where(rows == index[face : face + 1], factor[face : face + 1], 0.0)
        total += factor[face : face + 1]
    extended = jnp.concatenate([before_ref[...], flow, after_ref[...]], axis=0)
    w_hi, w_mid, _ = split3(weight)
    e_hi, e_mid, _ = split3(extended)
    dims = (((0,), (0,)), ((), ()))
    coupling = (
        lax.dot_general(w_hi, e_hi, dims, preferred_element_type=f32)
        + lax.dot_general(w_hi, e_mid, dims, preferred_element_type=f32)
        + lax.dot_general(w_mid, e_hi, dims, preferred_element_type=f32)
    )
    scale = time_step * coefficient_ref[...]
    spread = (flow + scale * coupling) / (1.0 + scale * column(total))
    spread_ref[...] = spread
    pack(send_ref, spread, heat_ref[:, 0:1], owner_ref[...], slot_ref[...], me)


def table(index_iota, first, second):
    one, zero = jnp.ones((), bf16), jnp.zeros((), bf16)
    return jnp.where(index_iota == first, one, zero) + jnp.where(index_iota == second, one, zero)


def newton_kernel(
    me_ref,
    recv_ref,
    spread_ref,
    heat_ref,
    owner_ref,
    slot_ref,
    frequency_ref,
    energy_ref,
    species_ref,
    out_ref,
    react_ref,
    react_t_ref,
    product_t_ref,
    initial_ref,
    loss_ref,
    gain_ref,
    log_ref,
):
    initial, heat = unpack(
        recv_ref,
        spread_ref[...],
        heat_ref[:, 0:1],
        owner_ref[...],
        slot_ref[...],
        me_ref[0],
    )
    inverse = 1.0 / heat
    initial_ref[...] = initial
    out_ref[...] = initial
    species = initial.shape[1]
    reactions = frequency_ref.shape[1]

    for turn in range(NEWTON):
        wanted = (512, 256, 128) if turn == 0 else (1536, 768, 512, 256, 128)
        block = next(b for b in wanted if reactions % b == 0)
        log_ref[...] = jnp.log(out_ref[...]).astype(bf16)
        loss_ref[...] = jnp.zeros_like(loss_ref)
        gain_ref[...] = jnp.zeros_like(gain_ref)
        if turn == 0:
            down_species = iota((species, block), 0).astype(i16)
            along_species = iota((block, species), 1).astype(i16)

        def add_block(b, carry):
            at = pl.ds(pl.multiple_of(b * block, block), block)
            if turn == 0:
                index = species_ref[:, at]
                columns = jnp.transpose(index).astype(i16)
                react_ref[:, at] = table(
                    down_species, index[0:1].astype(i16), index[1:2].astype(i16)
                )
                react_t_ref[at, :] = table(along_species, columns[:, 0:1], columns[:, 1:2])
                product_t_ref[at, :] = table(along_species, columns[:, 2:3], columns[:, 3:4])
            exponent = jnp.dot(log_ref[...], react_ref[:, at], preferred_element_type=f32)
            log_rate = frequency_ref[:, at] - energy_ref[:, at] * inverse
            rate = jnp.exp(log_rate + exponent).astype(bf16)
            loss_ref[...] += jnp.dot(rate, react_t_ref[at, :], preferred_element_type=f32)
            gain_ref[...] += jnp.dot(rate, product_t_ref[at, :], preferred_element_type=f32)
            return carry

        lax.fori_loop(0, reactions // block, add_block, 0)
        out_ref[...] = (initial_ref[...] + time_step * gain_ref[...]) / (
            1.0 + time_step * loss_ref[...] / out_ref[...]
        )


def call(kernel, inputs, outputs, scratch=(), limit=32):
    return pl.pallas_call(
        kernel,
        out_shape=tuple(jax.ShapeDtypeStruct(shape, f32) for shape in outputs),
        in_specs=[SMEM] + [VMEM] * (len(inputs) - 1),
        out_specs=tuple([VMEM] * len(outputs)),
        scratch_shapes=list(scratch),
        compiler_params=pltpu.CompilerParams(vmem_limit_bytes=limit * 2**20),
    )(*inputs)


def local(
    earlier_kinetics_concentrations,
    thermal_level,
    earlier_fluid_holder,
    earlier_fluid_slot,
    adjacent_volumes,
    interface_spreading_factor,
    species_spreading_coefficient,
    present_kinetics_holder,
    present_kinetics_slot,
    natural_frequency_factor,
    arrhenius_energy,
    consumed_species,
    yielded_species,
):
    n, species = earlier_kinetics_concentrations.shape
    reactions = natural_frequency_factor.shape[0]
    partners = lax.axis_size("cells")
    me = lax.axis_index("cells").astype(i32).reshape(1)
    row = lambda x: x.reshape(1, -1)
    temper, owner, slot = row(thermal_level), row(earlier_fluid_holder), row(earlier_fluid_slot)
    next_owner, next_slot = row(present_kinetics_holder), row(present_kinetics_slot)
    buffer = (partners, CAP, species + EXTRA)

    def exchange(x):
        return lax.all_to_all(x, "cells", split_axis=0, concat_axis=0, tiled=True)

    (send,) = call(
        pack_kernel, (me, earlier_kinetics_concentrations, temper, owner, slot), (buffer,)
    )
    flow, heat, last, first = call(
        flow_kernel,
        (me, exchange(send), earlier_kinetics_concentrations, temper, owner, slot),
        ((n, species), (n, EXTRA), (HALO, species), (HALO, species)),
    )
    up = [(i, i + 1) for i in range(partners - 1)]
    down = [(i + 1, i) for i in range(partners - 1)]
    before = lax.ppermute(last, "cells", up)
    after = lax.ppermute(first, "cells", down)
    spread, send = call(
        spread_kernel,
        (
            me,
            flow,
            heat,
            before,
            after,
            adjacent_volumes,
            interface_spreading_factor,
            row(species_spreading_coefficient),
            next_owner,
            next_slot,
        ),
        ((n, species), buffer),
    )
    index = jnp.concatenate(
        [consumed_species, yielded_species, jnp.zeros((4, reactions), i32)], axis=0
    )
    (chem_next,) = call(
        newton_kernel,
        (
            me,
            exchange(send),
            spread,
            heat,
            next_owner,
            next_slot,
            row(natural_frequency_factor),
            row(arrhenius_energy),
            index,
        ),
        ((n, species),),
        scratch=(
            pltpu.VMEM((species, reactions), bf16),
            pltpu.VMEM((reactions, species), bf16),
            pltpu.VMEM((reactions, species), bf16),
            pltpu.VMEM((n, species), f32),
            pltpu.VMEM((n, species), f32),
            pltpu.VMEM((n, species), f32),
            pltpu.VMEM((n, species), bf16),
        ),
        limit=62,
    )
    return (spread, chem_next)


def solution(mesh):
    in_specs = (
        P("cells", None),
        P("cells"),
        P("cells"),
        P("cells"),
        P(None, "cells"),
        P(None, "cells"),
        P(),
        P("cells"),
        P("cells"),
        P(),
        P(),
        P(),
        P(),
    )
    out_specs = (P("cells", None), P("cells", None))
    return jax.shard_map(local, mesh=mesh, in_specs=in_specs, out_specs=out_specs, check_vma=False)
```

```python
import functools

import jax
import jax.numpy as jnp
from jax import lax
from jax.experimental import pallas as pl
from jax.experimental.pallas import tpu as pltpu
from jax.sharding import PartitionSpec as P

NEWTON = 2
HALO = 32
CAP = 2
EXTRA = 128

time_step = 0.5

f32 = jnp.float32
bf16 = jnp.bfloat16
i32 = jnp.int32
i16 = jnp.int16

VMEM = pl.BlockSpec(memory_space=pltpu.VMEM)
SMEM = pl.BlockSpec(memory_space=pltpu.SMEM)
HBM = pl.BlockSpec(memory_space=pltpu.HBM)
ANY = pl.BlockSpec(memory_space=pl.ANY)


def iota(shape, dim):
    return lax.broadcasted_iota(i32, shape, dim)


def column(row):
    n = row.shape[1]
    eye = iota((n, n), 0) == iota((n, n), 1)
    return jnp.sum(jnp.where(eye, row, jnp.zeros_like(row)), axis=1, keepdims=True)


def split3(x):
    hi = x.astype(bf16)
    rest = x - hi.astype(f32)
    mid = rest.astype(bf16)
    lo = (rest - mid.astype(f32)).astype(bf16)
    return hi, mid, lo


def pick(choice, rows, dims=(((1,), (0,)), ((), ()))):
    choice = choice.astype(bf16)
    out = None
    for part in split3(rows):
        term = lax.dot_general(choice, part, dims, preferred_element_type=f32)
        out = term if out is None else out + term
    return out


def send_choice(owner, me, partners):
    n = owner.shape[1]
    hits = ((iota((partners, n), 0) == owner) & (owner != me)).astype(f32)
    before = (iota((n, n), 0) < iota((n, n), 1)).astype(bf16)
    earlier = jnp.dot(hits.astype(bf16), before, preferred_element_type=f32)
    within = jnp.sum(earlier * hits, axis=0, keepdims=True).astype(i32)
    position = jnp.where(owner != me, owner * CAP + within, -1)
    return (iota((partners * CAP, n), 0) == position).astype(f32)


def in_hbm(*arrays):
    return tuple(pltpu.with_memory_space_constraint(x, pltpu.HBM) for x in arrays)


def begin(sources, targets, sems):
    copies = [
        pltpu.make_async_copy(source, target, sems.at[i])
        for i, (source, target) in enumerate(zip(sources, targets))
    ]
    for copy in copies:
        copy.start()
    return copies


def finish(copies):
    for copy in copies:
        copy.wait()


def beside_rows(values):
    n = values[0].shape[1]
    lane = iota((n, EXTRA), 1)
    out = jnp.zeros((n, EXTRA), f32)
    for i, value in enumerate(values):
        out = jnp.where(lane == i, column(value.astype(f32)), out)
    return out


def flat(ref):
    return jnp.concatenate([ref[q : q + 1, :] for q in range(ref.shape[0])], axis=1)


def arrived(recv_ref, places, n):
    partners, cap, width = recv_ref.shape
    got = recv_ref[...].reshape(partners * cap, width)
    land = (iota((partners * cap, n), 1) == places.astype(i32) - 1).astype(f32)
    return pick(land, got, (((0,), (0,)), ((), ())))


def stay_choice(owner, slot, me):
    n = owner.shape[1]
    return ((iota((n, n), 0) == slot) & (owner == me)).astype(f32)


def pack_kernel(
    me_ref,
    rows_hbm,
    temper_hbm,
    owner_hbm,
    slot_hbm,
    next_owner_hbm,
    next_slot_hbm,
    send_ref,
    rows,
    temper,
    owner,
    slot,
    next_owner,
    next_slot,
    sems,
):
    sources = (temper_hbm, owner_hbm, slot_hbm, next_owner_hbm, next_slot_hbm, rows_hbm)
    copies = begin(sources, (temper, owner, slot, next_owner, next_slot, rows), sems)
    finish(copies[:-1])
    partners, cap, _ = send_ref.shape
    species = rows.shape[1]
    choice = send_choice(owner[...], me_ref[0], partners)
    next_choice = send_choice(next_owner[...], me_ref[0], partners)
    none = jnp.zeros_like(temper[...])
    beside = pick(choice, beside_rows((temper[...], slot[...] + 1, none))) + pick(
        next_choice, beside_rows((none, none, next_slot[...] + 1))
    )
    send_ref[:, :, species:] = beside.reshape(partners, cap, EXTRA)
    finish(copies[-1:])
    send_ref[:, :, :species] = pick(choice, rows[...]).reshape(partners, cap, species)


def prepare_kernel(
    me_ref,
    rows_hbm,
    temper_hbm,
    owner_hbm,
    slot_hbm,
    next_owner_hbm,
    adjacent_hbm,
    factor_hbm,
    coefficient_hbm,
    frequency_hbm,
    energy_hbm,
    consumed_hbm,
    after_ref,
    state_ref,
    heat_ref,
    choice_ref,
    weight_hi_ref,
    weight_mid_ref,
    scale_ref,
    total_ref,
    frequency_ref,
    energy_ref,
    consumed_ref,
    rows,
    temper,
    owner,
    slot,
    next_owner,
    adjacent,
    factor,
    coefficient,
    frequency,
    energy,
    sems,
):
    sources = (temper_hbm, owner_hbm, slot_hbm, next_owner_hbm, adjacent_hbm, factor_hbm)
    sources += (coefficient_hbm, frequency_hbm, energy_hbm, consumed_hbm, rows_hbm)
    targets = (temper, owner, slot, next_owner, adjacent, factor)
    targets += (coefficient, frequency, energy, consumed_ref, rows)
    copies = begin(sources, targets, sems)
    finish(copies[:-1])
    me = me_ref[0]
    choice_ref[...] = send_choice(next_owner[...], me, choice_ref.shape[0] // CAP)
    weight, total = face_weights(me, adjacent[...], factor[...])
    weight_hi_ref[...], weight_mid_ref[...], _ = split3(weight)
    scale_ref[...] = time_step * flat(coefficient)
    total_ref[...] = jnp.broadcast_to(column(total), total_ref.shape)
    frequency_ref[...] = flat(frequency)
    energy_ref[...] = flat(energy)
    stay = stay_choice(owner[...], slot[...], me)
    heat_ref[...] = pick(stay, jnp.broadcast_to(column(temper[...]), heat_ref.shape))
    finish(copies[-1:])
    state_ref[...] = pick(stay, rows[...])


def flow_kernel(
    me_ref,
    recv_ref,
    state_ref,
    temper_ref,
    after_ref,
    flow_ref,
    heat_ref,
    inner_ref,
    outer_ref,
    place_ref,
):
    n, species = state_ref.shape
    partners, cap, width = recv_ref.shape
    beside = recv_ref[:, :, species:].reshape(partners * cap, EXTRA)
    rows = arrived(recv_ref, beside[:, 1:2], n)
    state = rows[:, :species] + state_ref[...]
    flow_ref[...] = state
    heat_ref[...] = rows[:, species:] + temper_ref[...]
    place_ref[...] = jnp.broadcast_to(beside[:, 2:3], place_ref.shape)
    even = lax.rem(me_ref[0], 2) == 0
    inner_ref[...] = jnp.where(even, state[n - HALO :], state[:HALO])
    outer_ref[...] = jnp.where(even, state[:HALO], state[n - HALO :])


def face_weights(me, adjacent, factor):
    n = adjacent.shape[1]
    index = adjacent - me * n + HALO
    rows = iota((n + 2 * HALO, n), 0)
    weight = jnp.zeros((n + 2 * HALO, n), f32)
    total = jnp.zeros((1, n), f32)
    for face in range(adjacent.shape[0]):
        weight += jnp.where(rows == index[face : face + 1], factor[face : face + 1], 0.0)
        total += factor[face : face + 1]
    return weight, total


def table(index_iota, first, second):
    one, zero = jnp.ones((), bf16), jnp.zeros((), bf16)
    return jnp.where(index_iota == first, one, zero) + jnp.where(index_iota == second, one, zero)


def largest(total, *wanted):
    return next(b for b in wanted if total % b == 0)


def column_table(pairs):
    block = pairs.shape[1]
    columns = jnp.transpose(
        jnp.concatenate([pairs, jnp.zeros((6, block), i32)], axis=0)
    ).astype(i16)

    def rows(species):
        return table(
            iota((block, species), 1).astype(i16), columns[:, 0:1], columns[:, 1:2]
        )

    return rows


def product_kernel(yielded_ref, after_ref, product_t_ref, done_ref):
    product_t_ref[...] = column_table(yielded_ref[...])(product_t_ref.shape[1])
    done_ref[...] = jnp.zeros_like(done_ref)


def react_kernel(
    consumed_ref, product_t_hbm, after_ref, react_ref, react_t_ref, product_t_ref, sems
):
    copies = begin((product_t_hbm,), (product_t_ref,), sems)
    species, reactions = react_ref.shape
    block = largest(reactions, 512, 256, 128)
    down_species = iota((species, block), 0).astype(i16)

    def fill(b, carry):
        at = pl.ds(pl.multiple_of(b * block, block), block)
        used = consumed_ref[:, at]
        react_ref[:, at] = table(down_species, used[0:1].astype(i16), used[1:2].astype(i16))
        return carry

    def fill_t(b, carry):
        at = pl.ds(pl.multiple_of(b * block, block), block)
        react_t_ref[at, :] = column_table(consumed_ref[:, at])(species)
        return carry

    lax.fori_loop(0, reactions // block, fill, 0)
    lax.fori_loop(0, reactions // block, fill_t, 0, unroll=largest(reactions // block, 3, 2, 1))
    finish(copies)


def chemistry_kernel(
    me_ref,
    flow_ref,
    heat_ref,
    inner_ref,
    outer_ref,
    react_ref,
    react_t_ref,
    product_t_ref,
    choice_ref,
    weight_hi_ref,
    weight_mid_ref,
    scale_ref,
    total_ref,
    frequency_ref,
    energy_ref,
    spread_ref,
    chem_ref,
    send_ref,
    rate_ref,
    log_ref,
):
    flow = flow_ref[...]
    even = lax.rem(me_ref[0], 2) == 0
    inner, outer = inner_ref[...], outer_ref[...]
    extended = jnp.concatenate(
        [jnp.where(even, outer, inner), flow, jnp.where(even, inner, outer)], axis=0
    )
    e_hi, e_mid, _ = split3(extended)
    dims = (((0,), (0,)), ((), ()))
    coupling = (
        lax.dot_general(weight_hi_ref[...], e_hi, dims, preferred_element_type=f32)
        + lax.dot_general(weight_hi_ref[...], e_mid, dims, preferred_element_type=f32)
        + lax.dot_general(weight_mid_ref[...], e_hi, dims, preferred_element_type=f32)
    )
    scale = scale_ref[...]
    spread = (flow + scale * coupling) / (1.0 + scale * total_ref[:, 0:1])
    spread_ref[...] = spread
    chem_ref[...] = spread
    inverse = 1.0 / heat_ref[:, 0:1]
    species, reactions = react_ref.shape
    across = largest(reactions, 512, 256, 128)
    down = largest(species, 512, 256, 128)
    tiles = [slice(first, first + down) for first in range(0, species, down)]

    for turn in range(NEWTON):
        log_ref[...] = jnp.log(chem_ref[...]).astype(bf16)
        for first in range(0, reactions, across):
            at = slice(first, first + across)
            exponent = jnp.dot(log_ref[...], react_ref[:, at], preferred_element_type=f32)
            log_rate = frequency_ref[:, at] - energy_ref[:, at] * inverse
            rate_ref[:, at] = jnp.exp(log_rate + exponent).astype(bf16)
        for at in tiles:
            loss = jnp.dot(rate_ref[...], react_t_ref[:, at], preferred_element_type=f32)
            gain = jnp.dot(rate_ref[...], product_t_ref[:, at], preferred_element_type=f32)
            chem_ref[:, at] = (spread_ref[:, at] + time_step * gain) / (
                1.0 + time_step * loss / chem_ref[:, at]
            )
    send_ref[...] = pick(choice_ref[...], chem_ref[...]).reshape(send_ref.shape)


def stay_kernel(me_ref, rows_ref, owner_ref, slot_ref, out_ref):
    out_ref[...] = pick(stay_choice(owner_ref[...], slot_ref[...], me_ref[0]), rows_ref[...])


def land_kernel(recv_ref, place_ref, stay_ref, out_ref):
    out_ref[...] = arrived(recv_ref, place_ref[:, 0:1], out_ref.shape[0]) + stay_ref[...]


def call(kernel, inputs, specs, outputs, scratch=(), limit=6, cost=None):
    outputs = tuple(jax.ShapeDtypeStruct(o, f32) if isinstance(o, tuple) else o for o in outputs)
    return pl.pallas_call(
        kernel,
        out_shape=outputs,
        in_specs=specs,
        out_specs=tuple([VMEM] * len(outputs)),
        scratch_shapes=list(scratch),
        compiler_params=pltpu.CompilerParams(vmem_limit_bytes=limit * 2**20),
        cost_estimate=cost,
    )(*inputs)


def like(*arrays):
    return [pltpu.VMEM(x.shape, x.dtype) for x in arrays], pltpu.SemaphoreType.DMA((len(arrays),))


def table_cost(species, reactions, tables):
    return pl.CostEstimate(
        flops=40 * species * reactions * tables,
        bytes_accessed=2 * species * reactions * tables,
        transcendentals=0,
    )


def local(
    earlier_kinetics_concentrations,
    thermal_level,
    earlier_fluid_holder,
    earlier_fluid_slot,
    adjacent_volumes,
    interface_spreading_factor,
    species_spreading_coefficient,
    present_kinetics_holder,
    present_kinetics_slot,
    natural_frequency_factor,
    arrhenius_energy,
    consumed_species,
    yielded_species,
):
    n, species = earlier_kinetics_concentrations.shape
    reactions = natural_frequency_factor.shape[0]
    partners = lax.axis_size("cells")
    me = lax.axis_index("cells").astype(i32).reshape(1)
    row = lambda x: x.reshape(1, -1)

    def exchange(x):
        return lax.all_to_all(x, "cells", split_axis=0, concat_axis=0, tiled=True)

    earlier = (
        earlier_kinetics_concentrations,
        row(thermal_level),
        row(earlier_fluid_holder),
        row(earlier_fluid_slot),
    )
    owner, slot = row(present_kinetics_holder), row(present_kinetics_slot)
    pack_scratch, pack_sems = like(*earlier, owner, slot)
    (send,) = call(
        pack_kernel,
        (me, *in_hbm(*earlier, owner, slot)),
        [SMEM] + [HBM] * 6,
        ((partners, CAP, species + EXTRA),),
        [*pack_scratch, pack_sems],
    )

    block = largest(reactions, 512, 256, 128)
    product_t, done = pl.pallas_call(
        product_kernel,
        grid=(reactions // block,),
        out_shape=(
            pltpu.HBM((reactions, species), bf16),
            jax.ShapeDtypeStruct((8, 128), f32),
        ),
        in_specs=[pl.BlockSpec((2, block), lambda b: (0, b)), ANY],
        out_specs=(
            pl.BlockSpec((block, species), lambda b: (b, 0)),
            pl.BlockSpec((8, 128), lambda b: (0, 0)),
        ),
        compiler_params=pltpu.CompilerParams(vmem_limit_bytes=16 * 2**20),
        cost_estimate=table_cost(species, reactions, 1),
    )(*in_hbm(yielded_species), send)

    recv = exchange(send)
    ready = (
        owner,
        adjacent_volumes,
        interface_spreading_factor,
        species_spreading_coefficient.reshape(-1, 128),
        natural_frequency_factor.reshape(-1, 128),
        arrhenius_energy.reshape(-1, 128),
    )
    ready_scratch, _ = like(*earlier, *ready)
    state, heat, *prepared, consumed = call(
        prepare_kernel,
        (me, *in_hbm(*earlier, *ready, consumed_species), send),
        [SMEM] + [HBM] * 11 + [ANY],
        (
            (n, species),
            (n, EXTRA),
            (partners * CAP, n),
            jax.ShapeDtypeStruct((n + 2 * HALO, n), bf16),
            jax.ShapeDtypeStruct((n + 2 * HALO, n), bf16),
            (1, species),
            (n, 128),
            (1, reactions),
            (1, reactions),
            jax.ShapeDtypeStruct((2, reactions), i32),
        ),
        [*ready_scratch, pltpu.SemaphoreType.DMA((11,))],
    )
    flow, heat, to_inner, to_outer, place = call(
        flow_kernel,
        (me, recv, state, heat, done),
        [SMEM] + [VMEM] * 3 + [ANY],
        ((n, species), (n, EXTRA), (HALO, species), (HALO, species), (partners * CAP, EXTRA)),
    )
    inner = [(i, i ^ 1) for i in range(partners)]
    outer = [(i, ((i + 1) ^ 1) - 1) for i in range(1, partners - 1)]
    from_outer = lax.ppermute(to_outer, "cells", outer)
    from_inner = lax.ppermute(to_inner, "cells", inner)
    tables = call(
        react_kernel,
        (consumed, *in_hbm(product_t), heat),
        [VMEM, HBM, ANY],
        (
            jax.ShapeDtypeStruct((species, reactions), bf16),
            jax.ShapeDtypeStruct((reactions, species), bf16),
            jax.ShapeDtypeStruct((reactions, species), bf16),
        ),
        [pltpu.SemaphoreType.DMA((1,))],
        limit=4,
        cost=table_cost(species, reactions, 2),
    )
    spread, chem, send = call(
        chemistry_kernel,
        (me, flow, heat, from_inner, from_outer, *tables, *prepared),
        [SMEM] + [VMEM] * (7 + len(prepared)),
        ((n, species), (n, species), (partners, CAP, species)),
        [pltpu.VMEM((n, reactions), bf16), pltpu.VMEM((n, species), bf16)],
        limit=6,
    )
    recv = exchange(send)
    (stay,) = call(stay_kernel, (me, chem, owner, slot), [SMEM] + [VMEM] * 3, ((n, species),))
    (chem_next,) = call(land_kernel, (recv, place, stay), [VMEM] * 3, ((n, species),))
    return (spread, chem_next)


def solution(mesh):
    in_specs = (
        P("cells", None),
        P("cells"),
        P("cells"),
        P("cells"),
        P(None, "cells"),
        P(None, "cells"),
        P(),
        P("cells"),
        P("cells"),
        P(),
        P(),
        P(),
        P(),
    )
    out_specs = (P("cells", None), P("cells", None))
    return jax.shard_map(local, mesh=mesh, in_specs=in_specs, out_specs=out_specs, check_vma=False)
```

```python
import functools

import jax
import jax.numpy as jnp
from jax import lax
from jax.experimental import pallas as pl
from jax.experimental.pallas import tpu as pltpu
from jax.sharding import PartitionSpec as P

NEWTON = 2
HALO = 32
CAP = 2
EXTRA = 128

time_step = 0.5

f32 = jnp.float32
bf16 = jnp.bfloat16
i32 = jnp.int32
i16 = jnp.int16

VMEM = pl.BlockSpec(memory_space=pltpu.VMEM)
SMEM = pl.BlockSpec(memory_space=pltpu.SMEM)
HBM = pl.BlockSpec(memory_space=pltpu.HBM)
ANY = pl.BlockSpec(memory_space=pl.ANY)


def iota(shape, dim):
    return lax.broadcasted_iota(i32, shape, dim)


def largest(total, *wanted):
    return next(b for b in wanted if total % b == 0)


def column(row):
    n = row.shape[1]
    eye = iota((n, n), 0) == iota((n, n), 1)
    return jnp.sum(jnp.where(eye, row, jnp.zeros_like(row)), axis=1, keepdims=True)


def split(x):
    hi = x.astype(bf16)
    return hi, (x - hi.astype(f32)).astype(bf16)


def pick(choice, rows, dims=(((1,), (0,)), ((), ()))):
    choice = choice.astype(bf16)
    hi, mid = split(rows)
    return lax.dot_general(choice, hi, dims, preferred_element_type=f32) + lax.dot_general(
        choice, mid, dims, preferred_element_type=f32
    )


def send_choice(owner, me, partners):
    n = owner.shape[1]
    hits = ((iota((partners, n), 0) == owner) & (owner != me)).astype(f32)
    before = (iota((n, n), 0) < iota((n, n), 1)).astype(bf16)
    earlier = jnp.dot(hits.astype(bf16), before, preferred_element_type=f32)
    within = jnp.sum(earlier * hits, axis=0, keepdims=True).astype(i32)
    position = jnp.where(owner != me, owner * CAP + within, -1)
    return (iota((partners * CAP, n), 0) == position).astype(f32)


def in_hbm(*arrays):
    return tuple(pltpu.with_memory_space_constraint(x, pltpu.HBM) for x in arrays)


def begin(sources, targets, sems):
    copies = [
        pltpu.make_async_copy(source, target, sems.at[i])
        for i, (source, target) in enumerate(zip(sources, targets))
    ]
    for copy in copies:
        copy.start()
    return copies


def pieces(total):
    width = largest(total, 768, 512, 256, 128)
    return [slice(first, first + width) for first in range(0, total, width)]


def leave(source, target, sem):
    copy = pltpu.make_async_copy(source, target, sem)
    copy.start()
    return copy


def finish(copies):
    for copy in copies:
        copy.wait()


def beside_rows(values):
    n = values[0].shape[1]
    lane = iota((n, EXTRA), 1)
    out = jnp.zeros((n, EXTRA), f32)
    for i, value in enumerate(values):
        out = jnp.where(lane == i, column(value.astype(f32)), out)
    return out


def flat(ref):
    return jnp.concatenate([ref[q : q + 1, :] for q in range(ref.shape[0])], axis=1)


def landing(places, n):
    return (iota((places.shape[0], n), 1) == places.astype(i32) - 1).astype(f32)


def arrived(recv_ref, places, n):
    partners, cap, width = recv_ref.shape
    got = recv_ref[...].reshape(partners * cap, width)
    return pick(landing(places, n), got, (((0,), (0,)), ((), ())))


def stay_choice(owner, slot, me):
    n = owner.shape[1]
    return ((iota((n, n), 0) == slot) & (owner == me)).astype(f32)


def pack_kernel(
    me_ref,
    rows_hbm,
    temper_hbm,
    owner_hbm,
    slot_hbm,
    next_owner_hbm,
    next_slot_hbm,
    send_ref,
    rows,
    temper,
    owner,
    slot,
    next_owner,
    next_slot,
    sems,
):
    sources = (temper_hbm, owner_hbm, slot_hbm, next_owner_hbm, next_slot_hbm, rows_hbm)
    copies = begin(sources, (temper, owner, slot, next_owner, next_slot, rows), sems)
    finish(copies[:-1])
    partners, cap, _ = send_ref.shape
    species = rows.shape[1]
    choice = send_choice(owner[...], me_ref[0], partners)
    next_choice = send_choice(next_owner[...], me_ref[0], partners)
    none = jnp.zeros_like(temper[...])
    beside = pick(choice, beside_rows((temper[...], slot[...] + 1, none))) + pick(
        next_choice, beside_rows((none, none, next_slot[...] + 1))
    )
    send_ref[:, :, species:] = beside.reshape(partners, cap, EXTRA)
    finish(copies[-1:])
    send_ref[:, :, :species] = pick(choice, rows[...]).reshape(partners, cap, species)


def prepare_kernel(
    me_ref,
    rows_hbm,
    temper_hbm,
    owner_hbm,
    slot_hbm,
    next_owner_hbm,
    adjacent_hbm,
    factor_hbm,
    coefficient_hbm,
    frequency_hbm,
    energy_hbm,
    consumed_hbm,
    after_ref,
    state_ref,
    heat_ref,
    choice_ref,
    weight_hi_ref,
    weight_mid_ref,
    scale_ref,
    total_ref,
    frequency_ref,
    energy_ref,
    consumed_ref,
    rows,
    temper,
    owner,
    slot,
    next_owner,
    adjacent,
    factor,
    coefficient,
    frequency,
    energy,
    sems,
):
    sources = (temper_hbm, owner_hbm, slot_hbm, next_owner_hbm, adjacent_hbm, factor_hbm)
    sources += (coefficient_hbm, frequency_hbm, energy_hbm, consumed_hbm, rows_hbm)
    targets = (temper, owner, slot, next_owner, adjacent, factor)
    targets += (coefficient, frequency, energy, consumed_ref, rows)
    copies = begin(sources, targets, sems)
    finish(copies[:-1])
    me = me_ref[0]
    choice_ref[...] = send_choice(next_owner[...], me, choice_ref.shape[0] // CAP)
    weight, total = face_weights(me, adjacent[...], factor[...])
    weight_hi_ref[...], weight_mid_ref[...] = split(weight)
    scale_ref[...] = time_step * flat(coefficient)
    total_ref[...] = jnp.broadcast_to(column(total), total_ref.shape)
    frequency_ref[...] = flat(frequency)
    energy_ref[...] = flat(energy)
    stay = stay_choice(owner[...], slot[...], me)
    heat_ref[...] = pick(stay, jnp.broadcast_to(column(temper[...]), heat_ref.shape))
    finish(copies[-1:])
    state_ref[...] = pick(stay, rows[...])


def flow_kernel(
    me_ref,
    recv_ref,
    state_ref,
    temper_ref,
    after_ref,
    flow_ref,
    heat_ref,
    outer_ref,
    inner_ref,
    place_ref,
):
    n, species = state_ref.shape
    partners, cap, width = recv_ref.shape
    beside = recv_ref[:, :, species:].reshape(partners * cap, EXTRA)
    rows = arrived(recv_ref, beside[:, 1:2], n)
    state = rows[:, :species] + state_ref[...]
    flow_ref[...] = state
    heat_ref[...] = rows[:, species:] + temper_ref[...]
    place_ref[...] = jnp.broadcast_to(beside[:, 2:3], place_ref.shape)
    even = lax.rem(me_ref[0], 2) == 0
    inner_ref[...] = jnp.where(even, state[n - HALO :], state[:HALO])
    outer_ref[...] = jnp.where(even, state[:HALO], state[n - HALO :])


def face_weights(me, adjacent, factor):
    n = adjacent.shape[1]
    index = adjacent - me * n + HALO
    rows = iota((n + 2 * HALO, n), 0)
    weight = jnp.zeros((n + 2 * HALO, n), f32)
    total = jnp.zeros((1, n), f32)
    for face in range(adjacent.shape[0]):
        weight += jnp.where(rows == index[face : face + 1], factor[face : face + 1], 0.0)
        total += factor[face : face + 1]
    return weight, total


def table(index_iota, first, second):
    one, zero = jnp.ones((), bf16), jnp.zeros((), bf16)
    return jnp.where(index_iota == first, one, zero) + jnp.where(index_iota == second, one, zero)


def column_table(pairs):
    block = pairs.shape[1]
    columns = jnp.transpose(
        jnp.concatenate([pairs, jnp.zeros((6, block), i32)], axis=0)
    ).astype(i16)

    def rows(species):
        return table(
            iota((block, species), 1).astype(i16), columns[:, 0:1], columns[:, 1:2]
        )

    return rows


def product_kernel(
    yielded_hbm,
    consumed_hbm,
    after_hbm,
    product_t_hbm,
    head_hbm,
    done_ref,
    yielded,
    consumed,
    product_t,
    head,
    sems,
    out_sems,
):
    block, species = head.shape
    blocks = product_t.shape[0] // block
    finish(begin((yielded_hbm, consumed_hbm.at[:, :block]), (yielded, consumed), sems))

    def out(b):
        at = pl.ds(pl.multiple_of(b * block, block), block)
        return pltpu.make_async_copy(
            product_t.at[at, :], product_t_hbm.at[at, :], out_sems.at[b]
        )

    def fill(b, carry):
        at = pl.ds(pl.multiple_of(b * block, block), block)
        product_t[at, :] = column_table(yielded[:, at])(species)
        out(b).start()
        return carry

    def drain(b, carry):
        out(b).wait()
        return carry

    lax.fori_loop(0, blocks, fill, 0, unroll=largest(blocks, 3, 2, 1))
    head[...] = column_table(consumed[...])(species)
    left = leave(head, head_hbm, out_sems.at[blocks])
    done_ref[...] = jnp.zeros_like(done_ref)
    lax.fori_loop(0, blocks, drain, 0)
    left.wait()


def react_kernel(
    consumed_ref,
    product_t_hbm,
    head_hbm,
    after_ref,
    react_ref,
    react_t_ref,
    product_t_ref,
    sems,
):
    block = head_hbm.shape[0]
    targets = (product_t_ref, react_t_ref.at[:block, :])
    copies = begin((product_t_hbm, head_hbm), targets, sems)
    species, reactions = react_ref.shape
    down_species = iota((species, block), 0).astype(i16)

    def fill(b, carry):
        at = pl.ds(pl.multiple_of(b * block, block), block)
        used = consumed_ref[:, at]
        react_ref[:, at] = table(down_species, used[0:1].astype(i16), used[1:2].astype(i16))
        return carry

    def fill_t(b, carry):
        at = pl.ds(pl.multiple_of(b * block, block), block)
        react_t_ref[at, :] = column_table(consumed_ref[:, at])(species)
        return carry

    lax.fori_loop(0, reactions // block, fill, 0)
    rest = reactions // block - 1
    lax.fori_loop(1, rest + 1, fill_t, 0, unroll=largest(rest, 4, 3, 2, 1))
    finish(copies)


def chemistry_kernel(
    me_ref,
    flow_ref,
    heat_ref,
    inner_ref,
    outer_ref,
    react_ref,
    react_t_ref,
    product_t_ref,
    choice_ref,
    weight_hi_ref,
    weight_mid_ref,
    scale_ref,
    total_ref,
    frequency_ref,
    energy_ref,
    spread_hbm,
    chem_ref,
    send_hbm,
    rate_ref,
    log_ref,
    spread_ref,
    out_sems,
    *out,
):
    flow = flow_ref[...]
    even = lax.rem(me_ref[0], 2) == 0
    inner, outer = inner_ref[...], outer_ref[...]
    extended = jnp.concatenate(
        [jnp.where(even, outer, inner), flow, jnp.where(even, inner, outer)], axis=0
    )
    e_hi, e_mid = split(extended)
    dims = (((0,), (0,)), ((), ()))
    coupling = (
        lax.dot_general(weight_hi_ref[...], e_hi, dims, preferred_element_type=f32)
        + lax.dot_general(weight_hi_ref[...], e_mid, dims, preferred_element_type=f32)
        + lax.dot_general(weight_mid_ref[...], e_hi, dims, preferred_element_type=f32)
    )
    scale = scale_ref[...]
    spread = (flow + scale * coupling) / (1.0 + scale * total_ref[:, 0:1])
    spread_ref[...] = spread
    left = [leave(spread_ref, spread_hbm, out_sems.at[len(out)])]
    chem_ref[...] = spread
    inverse = 1.0 / heat_ref[:, 0:1]
    species, reactions = react_ref.shape
    across = largest(reactions, 512, 256, 128)
    down = largest(species, 512, 256, 128)
    tiles = [slice(first, first + down) for first in range(0, species, down)]

    for turn in range(NEWTON):
        log_ref[...] = jnp.log(chem_ref[...]).astype(bf16)
        for first in range(0, reactions, across):
            at = slice(first, first + across)
            exponent = jnp.dot(log_ref[...], react_ref[:, at], preferred_element_type=f32)
            log_rate = frequency_ref[:, at] - energy_ref[:, at] * inverse
            rate_ref[:, at] = jnp.exp(log_rate + exponent).astype(bf16)
        for at in tiles:
            loss = jnp.dot(rate_ref[...], react_t_ref[:, at], preferred_element_type=f32)
            gain = jnp.dot(rate_ref[...], product_t_ref[:, at], preferred_element_type=f32)
            chem_ref[:, at] = (spread_ref[:, at] + time_step * gain) / (
                1.0 + time_step * loss / chem_ref[:, at]
            )
    for i, at in enumerate(pieces(species)):
        out[i][...] = pick(choice_ref[...], chem_ref[:, at]).reshape(out[i].shape)
        left.append(leave(out[i], send_hbm.at[:, :, at], out_sems.at[i]))
    finish(left)


def stay_kernel(me_ref, rows_ref, place_ref, owner_ref, slot_ref, out_ref, land_ref):
    out_ref[...] = pick(stay_choice(owner_ref[...], slot_ref[...], me_ref[0]), rows_ref[...])
    land_ref[...] = jnp.transpose(landing(place_ref[:, 0:1], rows_ref.shape[0]))


def land_kernel(recv_ref, land_ref, stay_ref, out_hbm, out_sems, *out):
    partners, cap, species = recv_ref.shape
    left = []
    for i, at in enumerate(pieces(species)):
        got = recv_ref[:, :, at].reshape(partners * cap, -1)
        out[i][...] = pick(land_ref[...], got) + stay_ref[:, at]
        left.append(leave(out[i], out_hbm.at[:, at], out_sems.at[i]))
    finish(left)


def call(kernel, inputs, specs, outputs, scratch=(), limit=6, cost=None):
    outputs = tuple(jax.ShapeDtypeStruct(o, f32) if isinstance(o, tuple) else o for o in outputs)
    return pl.pallas_call(
        kernel,
        out_shape=outputs,
        in_specs=specs,
        out_specs=tuple(VMEM if isinstance(o, jax.ShapeDtypeStruct) else HBM for o in outputs),
        scratch_shapes=list(scratch),
        compiler_params=pltpu.CompilerParams(vmem_limit_bytes=limit * 2**20),
        cost_estimate=cost,
    )(*inputs)


def like(*arrays):
    return [pltpu.VMEM(x.shape, x.dtype) for x in arrays], pltpu.SemaphoreType.DMA((len(arrays),))


def table_cost(species, reactions, tables):
    return pl.CostEstimate(
        flops=40 * species * reactions * tables,
        bytes_accessed=2 * species * reactions * tables,
        transcendentals=0,
    )


def local(
    earlier_kinetics_concentrations,
    thermal_level,
    earlier_fluid_holder,
    earlier_fluid_slot,
    adjacent_volumes,
    interface_spreading_factor,
    species_spreading_coefficient,
    present_kinetics_holder,
    present_kinetics_slot,
    natural_frequency_factor,
    arrhenius_energy,
    consumed_species,
    yielded_species,
):
    n, species = earlier_kinetics_concentrations.shape
    reactions = natural_frequency_factor.shape[0]
    partners = lax.axis_size("cells")
    me = lax.axis_index("cells").astype(i32).reshape(1)
    row = lambda x: x.reshape(1, -1)

    def exchange(x):
        return lax.all_to_all(x, "cells", split_axis=0, concat_axis=0, tiled=True)

    earlier = (
        earlier_kinetics_concentrations,
        row(thermal_level),
        row(earlier_fluid_holder),
        row(earlier_fluid_slot),
    )
    owner, slot = row(present_kinetics_holder), row(present_kinetics_slot)
    pack_scratch, pack_sems = like(*earlier, owner, slot)
    parts = pieces(species)
    parts_scratch = [pltpu.VMEM((partners, CAP, species // len(parts)), f32) for _ in parts]
    (send,) = call(
        pack_kernel,
        (me, *in_hbm(*earlier, owner, slot)),
        [SMEM] + [HBM] * 6,
        ((partners, CAP, species + EXTRA),),
        [*pack_scratch, pack_sems],
    )

    block = largest(reactions, 512, 256, 128)
    product_t, head, done = call(
        product_kernel,
        in_hbm(yielded_species, consumed_species, send),
        [HBM] * 3,
        (
            pltpu.HBM((reactions, species), bf16),
            pltpu.HBM((block, species), bf16),
            (8, 128),
        ),
        [
            pltpu.VMEM((2, reactions), i32),
            pltpu.VMEM((2, block), i32),
            pltpu.VMEM((reactions, species), bf16),
            pltpu.VMEM((block, species), bf16),
            pltpu.SemaphoreType.DMA((2,)),
            pltpu.SemaphoreType.DMA((reactions // block + 1,)),
        ],
        limit=24,
        cost=table_cost(species, reactions, 1),
    )
    recv = exchange(send)
    ready = (
        owner,
        adjacent_volumes,
        interface_spreading_factor,
        species_spreading_coefficient.reshape(-1, 128),
        natural_frequency_factor.reshape(-1, 128),
        arrhenius_energy.reshape(-1, 128),
    )
    ready_scratch, _ = like(*earlier, *ready)
    state, heat, *prepared, consumed = call(
        prepare_kernel,
        (me, *in_hbm(*earlier, *ready, consumed_species, send)),
        [SMEM] + [HBM] * 12,
        (
            (n, species),
            (n, EXTRA),
            (partners * CAP, n),
            jax.ShapeDtypeStruct((n + 2 * HALO, n), bf16),
            jax.ShapeDtypeStruct((n + 2 * HALO, n), bf16),
            (1, species),
            (n, 128),
            (1, reactions),
            (1, reactions),
            jax.ShapeDtypeStruct((2, reactions), i32),
        ),
        [*ready_scratch, pltpu.SemaphoreType.DMA((11,))],
    )
    flow, heat, to_outer, to_inner, place = call(
        flow_kernel,
        (me, recv, state, heat, done),
        [SMEM] + [VMEM] * 3 + [ANY],
        ((n, species), (n, EXTRA), (HALO, species), (HALO, species), (partners * CAP, EXTRA)),
    )
    inner = [(i, i ^ 1) for i in range(partners)]
    outer = [(i, ((i + 1) ^ 1) - 1) for i in range(1, partners - 1)]
    from_outer = lax.ppermute(to_outer, "cells", outer)
    from_inner = lax.ppermute(to_inner, "cells", inner)
    tables = call(
        react_kernel,
        (consumed, *in_hbm(product_t, head), heat),
        [VMEM, HBM, HBM, ANY],
        (
            jax.ShapeDtypeStruct((species, reactions), bf16),
            jax.ShapeDtypeStruct((reactions, species), bf16),
            jax.ShapeDtypeStruct((reactions, species), bf16),
        ),
        [pltpu.SemaphoreType.DMA((2,))],
        limit=4,
        cost=table_cost(species, reactions, 2),
    )
    spread, chem, send = call(
        chemistry_kernel,
        (me, flow, heat, from_inner, from_outer, *tables, *prepared),
        [SMEM] + [VMEM] * (7 + len(prepared)),
        (
            pltpu.HBM((n, species), f32),
            (n, species),
            pltpu.HBM((partners, CAP, species), f32),
        ),
        [
            pltpu.VMEM((n, reactions), bf16),
            pltpu.VMEM((n, species), bf16),
            pltpu.VMEM((n, species), f32),
            pltpu.SemaphoreType.DMA((len(parts) + 1,)),
            *parts_scratch,
        ],
        limit=6,
    )
    recv = exchange(send)
    stay, land = call(
        stay_kernel,
        (me, chem, place, owner, slot),
        [SMEM] + [VMEM] * 4,
        ((n, species), (n, partners * CAP)),
    )
    (chem_next,) = call(
        land_kernel,
        (recv, land, stay),
        [VMEM] * 3,
        (pltpu.HBM((n, species), f32),),
        [
            pltpu.SemaphoreType.DMA((len(parts),)),
            *[pltpu.VMEM((n, species // len(parts)), f32) for _ in parts],
        ],
    )
    return (spread, chem_next)


def solution(mesh):
    in_specs = (
        P("cells", None),
        P("cells"),
        P("cells"),
        P("cells"),
        P(None, "cells"),
        P(None, "cells"),
        P(),
        P("cells"),
        P("cells"),
        P(),
        P(),
        P(),
        P(),
    )
    out_specs = (P("cells", None), P("cells", None))
    return jax.shard_map(local, mesh=mesh, in_specs=in_specs, out_specs=out_specs, check_vma=False)
```

```python
import functools

import jax
import jax.numpy as jnp
from jax import lax
from jax.experimental import pallas as pl
from jax.experimental.pallas import tpu as pltpu
from jax.sharding import PartitionSpec as P

NEWTON = 2
HALO = 32
CAP = 2
EXTRA = 128

time_step = 0.5

f32 = jnp.float32
bf16 = jnp.bfloat16
i32 = jnp.int32
i16 = jnp.int16

VMEM = pl.BlockSpec(memory_space=pltpu.VMEM)
SMEM = pl.BlockSpec(memory_space=pltpu.SMEM)
HBM = pl.BlockSpec(memory_space=pltpu.HBM)
ANY = pl.BlockSpec(memory_space=pl.ANY)


def iota(shape, dim):
    return lax.broadcasted_iota(i32, shape, dim)


def largest(total, *wanted):
    return next(b for b in wanted if total % b == 0)


def column(row):
    n = row.shape[1]
    eye = iota((n, n), 0) == iota((n, n), 1)
    return jnp.sum(jnp.where(eye, row, jnp.zeros_like(row)), axis=1, keepdims=True)


def split(x):
    hi = x.astype(bf16)
    return hi, (x - hi.astype(f32)).astype(bf16)


def pick(choice, rows, dims=(((1,), (0,)), ((), ()))):
    choice = choice.astype(bf16)
    hi, mid = split(rows)
    return lax.dot_general(choice, hi, dims, preferred_element_type=f32) + lax.dot_general(
        choice, mid, dims, preferred_element_type=f32
    )


def send_choice(owner, me, partners):
    n = owner.shape[1]
    hits = ((iota((partners, n), 0) == owner) & (owner != me)).astype(f32)
    before = (iota((n, n), 0) < iota((n, n), 1)).astype(bf16)
    earlier = jnp.dot(hits.astype(bf16), before, preferred_element_type=f32)
    within = jnp.sum(earlier * hits, axis=0, keepdims=True).astype(i32)
    position = jnp.where(owner != me, owner * CAP + within, -1)
    return (iota((partners * CAP, n), 0) == position).astype(f32)


def in_hbm(*arrays):
    return tuple(pltpu.with_memory_space_constraint(x, pltpu.HBM) for x in arrays)


def begin(sources, targets, sems):
    copies = [
        pltpu.make_async_copy(source, target, sems.at[i])
        for i, (source, target) in enumerate(zip(sources, targets))
    ]
    for copy in copies:
        copy.start()
    return copies


def pieces(total, *widths):
    width = largest(total, *widths, 256, 128)
    return [slice(first, first + width) for first in range(0, total, width)]


def leave(source, target, sem):
    copy = pltpu.make_async_copy(source, target, sem)
    copy.start()
    return copy


def finish(copies):
    for copy in copies:
        copy.wait()


def beside_rows(values):
    n = values[0].shape[1]
    lane = iota((n, EXTRA), 1)
    out = jnp.zeros((n, EXTRA), f32)
    for i, value in enumerate(values):
        out = jnp.where(lane == i, column(value.astype(f32)), out)
    return out


def flat(ref):
    return jnp.concatenate([ref[q : q + 1, :] for q in range(ref.shape[0])], axis=1)


def landing(places, n):
    return (iota((places.shape[0], n), 1) == places.astype(i32) - 1).astype(f32)


def arrived(recv_ref, places, n):
    partners, cap, width = recv_ref.shape
    got = recv_ref[...].reshape(partners * cap, width)
    return pick(landing(places, n), got, (((0,), (0,)), ((), ())))


def stay_choice(owner, slot, me):
    n = owner.shape[1]
    return ((iota((n, n), 0) == slot) & (owner == me)).astype(f32)


def pack_kernel(
    me_ref,
    rows_hbm,
    temper_hbm,
    owner_hbm,
    slot_hbm,
    next_owner_hbm,
    next_slot_hbm,
    send_ref,
    rows,
    temper,
    owner,
    slot,
    next_owner,
    next_slot,
    sems,
):
    sources = (temper_hbm, owner_hbm, slot_hbm, next_owner_hbm, next_slot_hbm, rows_hbm)
    copies = begin(sources, (temper, owner, slot, next_owner, next_slot, rows), sems)
    finish(copies[:-1])
    partners, cap, _ = send_ref.shape
    species = rows.shape[1]
    choice = send_choice(owner[...], me_ref[0], partners)
    next_choice = send_choice(next_owner[...], me_ref[0], partners)
    none = jnp.zeros_like(temper[...])
    beside = pick(choice, beside_rows((temper[...], slot[...] + 1, none))) + pick(
        next_choice, beside_rows((none, none, next_slot[...] + 1))
    )
    send_ref[:, :, species:] = beside.reshape(partners, cap, EXTRA)
    finish(copies[-1:])
    send_ref[:, :, :species] = pick(choice, rows[...]).reshape(partners, cap, species)


def prepare_kernel(
    me_ref,
    rows_hbm,
    temper_hbm,
    owner_hbm,
    slot_hbm,
    next_owner_hbm,
    adjacent_hbm,
    factor_hbm,
    coefficient_hbm,
    frequency_hbm,
    energy_hbm,
    consumed_hbm,
    after_ref,
    state_ref,
    heat_ref,
    choice_ref,
    weight_hi_ref,
    weight_mid_ref,
    scale_ref,
    total_ref,
    frequency_ref,
    energy_ref,
    consumed_ref,
    rows,
    temper,
    owner,
    slot,
    next_owner,
    adjacent,
    factor,
    coefficient,
    frequency,
    energy,
    sems,
):
    sources = (temper_hbm, owner_hbm, slot_hbm, next_owner_hbm, adjacent_hbm, factor_hbm)
    sources += (coefficient_hbm, frequency_hbm, energy_hbm, consumed_hbm, rows_hbm)
    targets = (temper, owner, slot, next_owner, adjacent, factor)
    targets += (coefficient, frequency, energy, consumed_ref, rows)
    copies = begin(sources, targets, sems)
    finish(copies[:-1])
    me = me_ref[0]
    choice_ref[...] = send_choice(next_owner[...], me, choice_ref.shape[0] // CAP)
    weight, total = face_weights(me, adjacent[...], factor[...])
    weight_hi_ref[...], weight_mid_ref[...] = split(weight)
    scale_ref[...] = time_step * flat(coefficient)
    total_ref[...] = jnp.broadcast_to(column(total), total_ref.shape)
    frequency_ref[...] = flat(frequency)
    energy_ref[...] = flat(energy)
    stay = stay_choice(owner[...], slot[...], me)
    heat_ref[...] = pick(stay, jnp.broadcast_to(column(temper[...]), heat_ref.shape))
    finish(copies[-1:])
    state_ref[...] = pick(stay, rows[...])


def flow_kernel(
    me_ref,
    recv_ref,
    state_ref,
    temper_ref,
    after_ref,
    flow_ref,
    heat_ref,
    outer_ref,
    inner_ref,
    place_ref,
):
    n, species = state_ref.shape
    partners, cap, width = recv_ref.shape
    beside = recv_ref[:, :, species:].reshape(partners * cap, EXTRA)
    rows = arrived(recv_ref, beside[:, 1:2], n)
    state = rows[:, :species] + state_ref[...]
    flow_ref[...] = state
    heat_ref[...] = rows[:, species:] + temper_ref[...]
    place_ref[...] = jnp.broadcast_to(beside[:, 2:3], place_ref.shape)
    even = lax.rem(me_ref[0], 2) == 0
    inner_ref[...] = jnp.where(even, state[n - HALO :], state[:HALO])
    outer_ref[...] = jnp.where(even, state[:HALO], state[n - HALO :])


def face_weights(me, adjacent, factor):
    n = adjacent.shape[1]
    index = adjacent - me * n + HALO
    rows = iota((n + 2 * HALO, n), 0)
    weight = jnp.zeros((n + 2 * HALO, n), f32)
    total = jnp.zeros((1, n), f32)
    for face in range(adjacent.shape[0]):
        weight += jnp.where(rows == index[face : face + 1], factor[face : face + 1], 0.0)
        total += factor[face : face + 1]
    return weight, total


def table(index_iota, first, second):
    one, zero = jnp.ones((), bf16), jnp.zeros((), bf16)
    return jnp.where(index_iota == first, one, zero) + jnp.where(index_iota == second, one, zero)


def column_table(pairs):
    block = pairs.shape[1]
    columns = jnp.transpose(
        jnp.concatenate([pairs, jnp.zeros((6, block), i32)], axis=0)
    ).astype(i16)

    def rows(species):
        return table(
            iota((block, species), 1).astype(i16), columns[:, 0:1], columns[:, 1:2]
        )

    return rows


def product_kernel(
    yielded_hbm,
    consumed_hbm,
    after_hbm,
    product_t_hbm,
    head_hbm,
    done_ref,
    yielded,
    consumed,
    product_t,
    head,
    sems,
    out_sems,
):
    reactions, species = product_t.shape
    block = largest(reactions, 512, 256, 128)
    blocks = reactions // block
    many = head.shape[0]
    finish(begin((yielded_hbm, consumed_hbm.at[:, :many]), (yielded, consumed), sems))

    def out(b):
        at = pl.ds(pl.multiple_of(b * block, block), block)
        return pltpu.make_async_copy(
            product_t.at[at, :], product_t_hbm.at[at, :], out_sems.at[b]
        )

    def fill(b, carry):
        at = pl.ds(pl.multiple_of(b * block, block), block)
        product_t[at, :] = column_table(yielded[:, at])(species)
        out(b).start()
        return carry

    def drain(b, carry):
        out(b).wait()
        return carry

    lax.fori_loop(0, blocks, fill, 0, unroll=largest(blocks, 3, 2, 1))
    for first in range(0, many, block):
        at = slice(first, first + block)
        head[at, :] = column_table(consumed[:, at])(species)
    left = leave(head, head_hbm, out_sems.at[blocks])
    done_ref[...] = jnp.zeros_like(done_ref)
    lax.fori_loop(0, blocks, drain, 0)
    left.wait()


def react_kernel(
    consumed_ref,
    product_t_hbm,
    head_hbm,
    after_ref,
    react_ref,
    react_t_ref,
    product_t_ref,
    sems,
):
    many = head_hbm.shape[0]
    targets = (product_t_ref, react_t_ref.at[:many, :])
    copies = begin((product_t_hbm, head_hbm), targets, sems)
    species, reactions = react_ref.shape
    block = largest(reactions, 512, 256, 128)
    down_species = iota((species, block), 0).astype(i16)

    def fill(b, carry):
        at = pl.ds(pl.multiple_of(b * block, block), block)
        used = consumed_ref[:, at]
        react_ref[:, at] = table(down_species, used[0:1].astype(i16), used[1:2].astype(i16))
        return carry

    def fill_t(b, carry):
        at = pl.ds(pl.multiple_of(b * block, block), block)
        react_t_ref[at, :] = column_table(consumed_ref[:, at])(species)
        return carry

    lax.fori_loop(0, reactions // block, fill, 0)
    blocks = reactions // block
    odd = many // block + (blocks - many // block) % 3
    lax.fori_loop(many // block, odd, fill_t, 0)
    lax.fori_loop(odd, blocks, fill_t, 0, unroll=3)
    finish(copies)


def chemistry_kernel(
    me_ref,
    flow_ref,
    heat_ref,
    inner_ref,
    outer_ref,
    react_ref,
    react_t_ref,
    product_t_ref,
    choice_ref,
    weight_hi_ref,
    weight_mid_ref,
    scale_ref,
    total_ref,
    frequency_ref,
    energy_ref,
    spread_hbm,
    chem_ref,
    send_hbm,
    rate_ref,
    log_ref,
    spread_ref,
    out_sems,
    *out,
):
    flow = flow_ref[...]
    even = lax.rem(me_ref[0], 2) == 0
    inner, outer = inner_ref[...], outer_ref[...]
    extended = jnp.concatenate(
        [jnp.where(even, outer, inner), flow, jnp.where(even, inner, outer)], axis=0
    )
    e_hi, e_mid = split(extended)
    dims = (((0,), (0,)), ((), ()))
    coupling = (
        lax.dot_general(weight_hi_ref[...], e_hi, dims, preferred_element_type=f32)
        + lax.dot_general(weight_hi_ref[...], e_mid, dims, preferred_element_type=f32)
        + lax.dot_general(weight_mid_ref[...], e_hi, dims, preferred_element_type=f32)
    )
    scale = scale_ref[...]
    spread = (flow + scale * coupling) / (1.0 + scale * total_ref[:, 0:1])
    spread_ref[...] = spread
    left = [leave(spread_ref, spread_hbm, out_sems.at[len(out)])]
    chem_ref[...] = spread
    inverse = 1.0 / heat_ref[:, 0:1]
    species, reactions = react_ref.shape
    across = largest(reactions, 512, 256, 128)
    down = largest(species, 512, 256, 128)
    tiles = [slice(first, first + down) for first in range(0, species, down)]

    for turn in range(NEWTON):
        log_ref[...] = jnp.log(chem_ref[...]).astype(bf16)
        for first in range(0, reactions, across):
            at = slice(first, first + across)
            exponent = jnp.dot(log_ref[...], react_ref[:, at], preferred_element_type=f32)
            log_rate = frequency_ref[:, at] - energy_ref[:, at] * inverse
            rate_ref[:, at] = jnp.exp(log_rate + exponent).astype(bf16)
        for at in tiles:
            loss = jnp.dot(rate_ref[...], react_t_ref[:, at], preferred_element_type=f32)
            gain = jnp.dot(rate_ref[...], product_t_ref[:, at], preferred_element_type=f32)
            chem_ref[:, at] = (spread_ref[:, at] + time_step * gain) / (
                1.0 + time_step * loss / chem_ref[:, at]
            )
    for i, at in enumerate(pieces(species, 768, 512)):
        out[i][...] = pick(choice_ref[...], chem_ref[:, at]).reshape(out[i].shape)
        left.append(leave(out[i], send_hbm.at[:, :, at], out_sems.at[i]))
    finish(left)


def stay_kernel(me_ref, rows_ref, place_ref, owner_ref, slot_ref, out_ref, land_ref):
    out_ref[...] = pick(stay_choice(owner_ref[...], slot_ref[...], me_ref[0]), rows_ref[...])
    land_ref[...] = jnp.transpose(landing(place_ref[:, 0:1], rows_ref.shape[0]))


def land_kernel(recv_ref, land_ref, stay_ref, out_hbm, out_sems, *out):
    partners, cap, species = recv_ref.shape
    left = []
    for i, at in enumerate(pieces(species, 384)):
        got = recv_ref[:, :, at].reshape(partners * cap, -1)
        out[i][...] = pick(land_ref[...], got) + stay_ref[:, at]
        left.append(leave(out[i], out_hbm.at[:, at], out_sems.at[i]))
    finish(left)


def call(kernel, inputs, specs, outputs, scratch=(), limit=6, cost=None):
    outputs = tuple(jax.ShapeDtypeStruct(o, f32) if isinstance(o, tuple) else o for o in outputs)
    return pl.pallas_call(
        kernel,
        out_shape=outputs,
        in_specs=specs,
        out_specs=tuple(VMEM if isinstance(o, jax.ShapeDtypeStruct) else HBM for o in outputs),
        scratch_shapes=list(scratch),
        compiler_params=pltpu.CompilerParams(vmem_limit_bytes=limit * 2**20),
        cost_estimate=cost,
    )(*inputs)


def like(*arrays):
    return [pltpu.VMEM(x.shape, x.dtype) for x in arrays], pltpu.SemaphoreType.DMA((len(arrays),))


def table_cost(species, reactions, tables):
    return pl.CostEstimate(
        flops=40 * species * reactions * tables,
        bytes_accessed=2 * species * reactions * tables,
        transcendentals=0,
    )


def local(
    earlier_kinetics_concentrations,
    thermal_level,
    earlier_fluid_holder,
    earlier_fluid_slot,
    adjacent_volumes,
    interface_spreading_factor,
    species_spreading_coefficient,
    present_kinetics_holder,
    present_kinetics_slot,
    natural_frequency_factor,
    arrhenius_energy,
    consumed_species,
    yielded_species,
):
    n, species = earlier_kinetics_concentrations.shape
    reactions = natural_frequency_factor.shape[0]
    partners = lax.axis_size("cells")
    me = lax.axis_index("cells").astype(i32).reshape(1)
    row = lambda x: x.reshape(1, -1)

    def exchange(x):
        return lax.all_to_all(x, "cells", split_axis=0, concat_axis=0, tiled=True)

    earlier = (
        earlier_kinetics_concentrations,
        row(thermal_level),
        row(earlier_fluid_holder),
        row(earlier_fluid_slot),
    )
    owner, slot = row(present_kinetics_holder), row(present_kinetics_slot)
    pack_scratch, pack_sems = like(*earlier, owner, slot)
    parts = pieces(species, 768, 512)
    parts_scratch = [pltpu.VMEM((partners, CAP, species // len(parts)), f32) for _ in parts]
    (send,) = call(
        pack_kernel,
        (me, *in_hbm(*earlier, owner, slot)),
        [SMEM] + [HBM] * 6,
        ((partners, CAP, species + EXTRA),),
        [*pack_scratch, pack_sems],
    )

    block = largest(reactions, 512, 256, 128)
    product_t, head, done = call(
        product_kernel,
        in_hbm(yielded_species, consumed_species, send),
        [HBM] * 3,
        (
            pltpu.HBM((reactions, species), bf16),
            pltpu.HBM((2 * block, species), bf16),
            (8, 128),
        ),
        [
            pltpu.VMEM((2, reactions), i32),
            pltpu.VMEM((2, 2 * block), i32),
            pltpu.VMEM((reactions, species), bf16),
            pltpu.VMEM((2 * block, species), bf16),
            pltpu.SemaphoreType.DMA((2,)),
            pltpu.SemaphoreType.DMA((reactions // block + 1,)),
        ],
        limit=24,
        cost=table_cost(species, reactions, 1),
    )
    recv = exchange(send)
    ready = (
        owner,
        adjacent_volumes,
        interface_spreading_factor,
        species_spreading_coefficient.reshape(-1, 128),
        natural_frequency_factor.reshape(-1, 128),
        arrhenius_energy.reshape(-1, 128),
    )
    ready_scratch, _ = like(*earlier, *ready)
    state, heat, *prepared, consumed = call(
        prepare_kernel,
        (me, *in_hbm(*earlier, *ready, consumed_species, send)),
        [SMEM] + [HBM] * 12,
        (
            (n, species),
            (n, EXTRA),
            (partners * CAP, n),
            jax.ShapeDtypeStruct((n + 2 * HALO, n), bf16),
            jax.ShapeDtypeStruct((n + 2 * HALO, n), bf16),
            (1, species),
            (n, 128),
            (1, reactions),
            (1, reactions),
            jax.ShapeDtypeStruct((2, reactions), i32),
        ),
        [*ready_scratch, pltpu.SemaphoreType.DMA((11,))],
    )
    flow, heat, to_outer, to_inner, place = call(
        flow_kernel,
        (me, recv, state, heat, done),
        [SMEM] + [VMEM] * 3 + [ANY],
        ((n, species), (n, EXTRA), (HALO, species), (HALO, species), (partners * CAP, EXTRA)),
    )
    inner = [(i, i ^ 1) for i in range(partners)]
    outer = [(i, ((i + 1) ^ 1) - 1) for i in range(1, partners - 1)]
    from_inner = lax.ppermute(to_inner, "cells", inner)
    from_outer = lax.ppermute(to_outer, "cells", outer)
    tables = call(
        react_kernel,
        (consumed, *in_hbm(product_t, head), heat),
        [VMEM, HBM, HBM, ANY],
        (
            jax.ShapeDtypeStruct((species, reactions), bf16),
            jax.ShapeDtypeStruct((reactions, species), bf16),
            jax.ShapeDtypeStruct((reactions, species), bf16),
        ),
        [pltpu.SemaphoreType.DMA((2,))],
        limit=4,
        cost=table_cost(species, reactions, 2),
    )
    spread, chem, send = call(
        chemistry_kernel,
        (me, flow, heat, from_inner, from_outer, *tables, *prepared),
        [SMEM] + [VMEM] * (7 + len(prepared)),
        (
            pltpu.HBM((n, species), f32),
            (n, species),
            pltpu.HBM((partners, CAP, species), f32),
        ),
        [
            pltpu.VMEM((n, reactions), bf16),
            pltpu.VMEM((n, species), bf16),
            pltpu.VMEM((n, species), f32),
            pltpu.SemaphoreType.DMA((len(parts) + 1,)),
            *parts_scratch,
        ],
        limit=6,
    )
    recv = exchange(send)
    stay, land = call(
        stay_kernel,
        (me, chem, place, owner, slot),
        [SMEM] + [VMEM] * 4,
        ((n, species), (n, partners * CAP)),
    )
    ends = pieces(species, 384)
    (chem_next,) = call(
        land_kernel,
        (recv, land, stay),
        [VMEM] * 3,
        (pltpu.HBM((n, species), f32),),
        [
            pltpu.SemaphoreType.DMA((len(ends),)),
            *[pltpu.VMEM((n, species // len(ends)), f32) for _ in ends],
        ],
    )
    return (spread, chem_next)


def solution(mesh):
    in_specs = (
        P("cells", None),
        P("cells"),
        P("cells"),
        P("cells"),
        P(None, "cells"),
        P(None, "cells"),
        P(),
        P("cells"),
        P("cells"),
        P(),
        P(),
        P(),
        P(),
    )
    out_specs = (P("cells", None), P("cells", None))
    return jax.shard_map(local, mesh=mesh, in_specs=in_specs, out_specs=out_specs, check_vma=False)
```

```python
import functools

import jax
import jax.numpy as jnp
from jax import lax
from jax.experimental import pallas as pl
from jax.experimental.pallas import tpu as pltpu
from jax.sharding import PartitionSpec as P

NEWTON = 2
HALO = 32
CAP = 2
EXTRA = 128

time_step = 0.5

f32 = jnp.float32
bf16 = jnp.bfloat16
i32 = jnp.int32
i16 = jnp.int16

VMEM = pl.BlockSpec(memory_space=pltpu.VMEM)
SMEM = pl.BlockSpec(memory_space=pltpu.SMEM)
HBM = pl.BlockSpec(memory_space=pltpu.HBM)
ANY = pl.BlockSpec(memory_space=pl.ANY)


def iota(shape, dim):
    return lax.broadcasted_iota(i32, shape, dim)


def largest(total, *wanted):
    return next(b for b in wanted if total % b == 0)


def column(row):
    n = row.shape[1]
    eye = iota((n, n), 0) == iota((n, n), 1)
    return jnp.sum(jnp.where(eye, row, jnp.zeros_like(row)), axis=1, keepdims=True)


def split(x):
    hi = x.astype(bf16)
    return hi, (x - hi.astype(f32)).astype(bf16)


def pick(choice, rows, dims=(((1,), (0,)), ((), ()))):
    choice = choice.astype(bf16)
    hi, mid = split(rows)
    return lax.dot_general(choice, hi, dims, preferred_element_type=f32) + lax.dot_general(
        choice, mid, dims, preferred_element_type=f32
    )


def send_choice(owner, me, partners):
    n = owner.shape[1]
    hits = ((iota((partners, n), 0) == owner) & (owner != me)).astype(f32)
    before = (iota((n, n), 0) < iota((n, n), 1)).astype(bf16)
    earlier = jnp.dot(hits.astype(bf16), before, preferred_element_type=f32)
    within = jnp.sum(earlier * hits, axis=0, keepdims=True).astype(i32)
    position = jnp.where(owner != me, owner * CAP + within, -1)
    return (iota((partners * CAP, n), 0) == position).astype(f32)


def in_hbm(*arrays):
    return tuple(pltpu.with_memory_space_constraint(x, pltpu.HBM) for x in arrays)


def begin(sources, targets, sems):
    copies = [
        pltpu.make_async_copy(source, target, sems.at[i])
        for i, (source, target) in enumerate(zip(sources, targets))
    ]
    for copy in copies:
        copy.start()
    return copies


def folds(total):
    width = total // 4 if total % 512 == 0 else total
    return [slice(first, first + width) for first in range(0, total, width)]


def leave(source, target, sem):
    copy = pltpu.make_async_copy(source, target, sem)
    copy.start()
    return copy


def finish(copies):
    for copy in copies:
        copy.wait()


def beside_rows(values):
    n = values[0].shape[1]
    lane = iota((n, EXTRA), 1)
    out = jnp.zeros((n, EXTRA), f32)
    for i, value in enumerate(values):
        out = jnp.where(lane == i, column(value.astype(f32)), out)
    return out


def flat(ref):
    return jnp.concatenate([ref[q : q + 1, :] for q in range(ref.shape[0])], axis=1)


def landing(places, n):
    return (iota((places.shape[0], n), 1) == places.astype(i32) - 1).astype(f32)


def arrived(recv_ref, places, n):
    partners, cap, width = recv_ref.shape
    got = recv_ref[...].reshape(partners * cap, width)
    return pick(landing(places, n), got, (((0,), (0,)), ((), ())))


def stay_choice(owner, slot, me):
    n = owner.shape[1]
    return ((iota((n, n), 0) == slot) & (owner == me)).astype(f32)


def pack_kernel(
    me_ref,
    rows_hbm,
    temper_hbm,
    owner_hbm,
    slot_hbm,
    next_owner_hbm,
    next_slot_hbm,
    send_ref,
    rows,
    temper,
    owner,
    slot,
    next_owner,
    next_slot,
    sems,
):
    sources = (temper_hbm, owner_hbm, slot_hbm, next_owner_hbm, next_slot_hbm, rows_hbm)
    copies = begin(sources, (temper, owner, slot, next_owner, next_slot, rows), sems)
    finish(copies[:-1])
    partners, cap, _ = send_ref.shape
    species = rows.shape[1]
    choice = send_choice(owner[...], me_ref[0], partners)
    next_choice = send_choice(next_owner[...], me_ref[0], partners)
    none = jnp.zeros_like(temper[...])
    beside = pick(choice, beside_rows((temper[...], slot[...] + 1, none))) + pick(
        next_choice, beside_rows((none, none, next_slot[...] + 1))
    )
    send_ref[:, :, species:] = beside.reshape(partners, cap, EXTRA)
    finish(copies[-1:])
    send_ref[:, :, :species] = pick(choice, rows[...]).reshape(partners, cap, species)


def prepare_kernel(
    me_ref,
    rows_hbm,
    temper_hbm,
    owner_hbm,
    slot_hbm,
    next_owner_hbm,
    adjacent_hbm,
    factor_hbm,
    coefficient_hbm,
    frequency_hbm,
    energy_hbm,
    consumed_hbm,
    after_ref,
    state_ref,
    heat_ref,
    choice_ref,
    weight_hi_ref,
    weight_mid_ref,
    scale_ref,
    total_ref,
    frequency_ref,
    energy_ref,
    consumed_ref,
    rows,
    temper,
    owner,
    slot,
    next_owner,
    adjacent,
    factor,
    coefficient,
    frequency,
    energy,
    sems,
):
    sources = (temper_hbm, owner_hbm, slot_hbm, next_owner_hbm, adjacent_hbm, factor_hbm)
    sources += (coefficient_hbm, frequency_hbm, energy_hbm, consumed_hbm, rows_hbm)
    targets = (temper, owner, slot, next_owner, adjacent, factor)
    targets += (coefficient, frequency, energy, consumed_ref, rows)
    copies = begin(sources, targets, sems)
    finish(copies[:-1])
    me = me_ref[0]
    choice_ref[...] = send_choice(next_owner[...], me, choice_ref.shape[0] // CAP)
    weight, total = face_weights(me, adjacent[...], factor[...])
    weight_hi_ref[...], weight_mid_ref[...] = split(weight)
    scale_ref[...] = time_step * flat(coefficient)
    total_ref[...] = jnp.broadcast_to(column(total), total_ref.shape)
    frequency_ref[...] = flat(frequency)
    energy_ref[...] = flat(energy)
    stay = stay_choice(owner[...], slot[...], me)
    heat_ref[...] = pick(stay, jnp.broadcast_to(column(temper[...]), heat_ref.shape))
    finish(copies[-1:])
    state_ref[...] = pick(stay, rows[...])


def flow_kernel(
    me_ref,
    recv_ref,
    state_ref,
    temper_ref,
    after_ref,
    flow_ref,
    heat_ref,
    outer_ref,
    inner_ref,
    place_ref,
):
    n, species = state_ref.shape
    partners, cap, width = recv_ref.shape
    beside = recv_ref[:, :, species:].reshape(partners * cap, EXTRA)
    rows = arrived(recv_ref, beside[:, 1:2], n)
    state = rows[:, :species] + state_ref[...]
    flow_ref[...] = state
    heat_ref[...] = rows[:, species:] + temper_ref[...]
    place_ref[...] = jnp.broadcast_to(beside[:, 2:3], place_ref.shape)
    even = lax.rem(me_ref[0], 2) == 0
    inner_ref[...] = jnp.where(even, state[n - HALO :], state[:HALO])
    outer_ref[...] = jnp.where(even, state[:HALO], state[n - HALO :])


def face_weights(me, adjacent, factor):
    n = adjacent.shape[1]
    index = adjacent - me * n + HALO
    rows = iota((n + 2 * HALO, n), 0)
    weight = jnp.zeros((n + 2 * HALO, n), f32)
    total = jnp.zeros((1, n), f32)
    for face in range(adjacent.shape[0]):
        weight += jnp.where(rows == index[face : face + 1], factor[face : face + 1], 0.0)
        total += factor[face : face + 1]
    return weight, total


def table(index_iota, first, second):
    one, zero = jnp.ones((), bf16), jnp.zeros((), bf16)
    return jnp.where(index_iota == first, one, zero) + jnp.where(index_iota == second, one, zero)


def column_table(pairs):
    block = pairs.shape[1]
    columns = jnp.transpose(
        jnp.concatenate([pairs, jnp.zeros((6, block), i32)], axis=0)
    ).astype(i16)

    def rows(species):
        return table(
            iota((block, species), 1).astype(i16), columns[:, 0:1], columns[:, 1:2]
        )

    return rows


def product_kernel(
    yielded_hbm,
    consumed_hbm,
    after_hbm,
    product_t_hbm,
    head_hbm,
    done_ref,
    yielded,
    consumed,
    product_t,
    head,
    sems,
    out_sems,
):
    reactions, species = product_t.shape
    block = largest(reactions, 512, 256, 128)
    blocks = reactions // block
    many = head.shape[0]
    finish(begin((yielded_hbm, consumed_hbm.at[:, :many]), (yielded, consumed), sems))

    def out(b):
        at = pl.ds(pl.multiple_of(b * block, block), block)
        return pltpu.make_async_copy(
            product_t.at[at, :], product_t_hbm.at[at, :], out_sems.at[b]
        )

    def fill(b, carry):
        at = pl.ds(pl.multiple_of(b * block, block), block)
        product_t[at, :] = column_table(yielded[:, at])(species)
        out(b).start()
        return carry

    def drain(b, carry):
        out(b).wait()
        return carry

    lax.fori_loop(0, blocks, fill, 0, unroll=largest(blocks, 3, 2, 1))
    for first in range(0, many, block):
        at = slice(first, first + block)
        head[at, :] = column_table(consumed[:, at])(species)
    left = leave(head, head_hbm, out_sems.at[blocks])
    done_ref[...] = jnp.zeros_like(done_ref)
    lax.fori_loop(0, blocks, drain, 0)
    left.wait()


def react_kernel(
    consumed_ref,
    product_t_hbm,
    head_hbm,
    after_ref,
    react_ref,
    react_t_ref,
    product_t_ref,
    sems,
):
    many = head_hbm.shape[0]
    targets = (product_t_ref, react_t_ref.at[:many, :])
    copies = begin((product_t_hbm, head_hbm), targets, sems)
    species, reactions = react_ref.shape
    block = largest(reactions, 512, 256, 128)
    down_species = iota((species, block), 0).astype(i16)

    def fill(b, carry):
        at = pl.ds(pl.multiple_of(b * block, block), block)
        used = consumed_ref[:, at]
        react_ref[:, at] = table(down_species, used[0:1].astype(i16), used[1:2].astype(i16))
        return carry

    def fill_t(b, carry):
        at = pl.ds(pl.multiple_of(b * block, block), block)
        react_t_ref[at, :] = column_table(consumed_ref[:, at])(species)
        return carry

    lax.fori_loop(0, reactions // block, fill, 0)
    blocks = reactions // block
    odd = many // block + (blocks - many // block) % 3
    lax.fori_loop(many // block, odd, fill_t, 0)
    lax.fori_loop(odd, blocks, fill_t, 0, unroll=3)
    finish(copies)


def chemistry_kernel(
    me_ref,
    flow_ref,
    heat_ref,
    inner_ref,
    outer_ref,
    react_ref,
    react_t_ref,
    product_t_ref,
    choice_ref,
    weight_hi_ref,
    weight_mid_ref,
    scale_ref,
    total_ref,
    frequency_ref,
    energy_ref,
    spread_hbm,
    chem_ref,
    send_hbm,
    rate_ref,
    log_ref,
    spread_ref,
    out_sems,
    *out,
):
    flow = flow_ref[...]
    even = lax.rem(me_ref[0], 2) == 0
    inner, outer = inner_ref[...], outer_ref[...]
    extended = jnp.concatenate(
        [jnp.where(even, outer, inner), flow, jnp.where(even, inner, outer)], axis=0
    )
    e_hi, e_mid = split(extended)
    dims = (((0,), (0,)), ((), ()))
    coupling = (
        lax.dot_general(weight_hi_ref[...], e_hi, dims, preferred_element_type=f32)
        + lax.dot_general(weight_hi_ref[...], e_mid, dims, preferred_element_type=f32)
        + lax.dot_general(weight_mid_ref[...], e_hi, dims, preferred_element_type=f32)
    )
    scale = scale_ref[...]
    spread = (flow + scale * coupling) / (1.0 + scale * total_ref[:, 0:1])
    spread_ref[...] = spread
    left = [leave(spread_ref, spread_hbm, out_sems.at[len(out)])]
    chem_ref[...] = spread
    inverse = 1.0 / heat_ref[:, 0:1]
    species, reactions = react_ref.shape
    across = largest(reactions, 512, 256, 128)
    down = largest(species, 512, 256, 128)
    tiles = [slice(first, first + down) for first in range(0, species, down)]

    for turn in range(NEWTON):
        log_ref[...] = jnp.log(chem_ref[...]).astype(bf16)
        for first in range(0, reactions, across):
            at = slice(first, first + across)
            exponent = jnp.dot(log_ref[...], react_ref[:, at], preferred_element_type=f32)
            log_rate = frequency_ref[:, at] - energy_ref[:, at] * inverse
            rate_ref[:, at] = jnp.exp(log_rate + exponent).astype(bf16)
        for at in tiles:
            loss = jnp.dot(rate_ref[...], react_t_ref[:, at], preferred_element_type=f32)
            gain = jnp.dot(rate_ref[...], product_t_ref[:, at], preferred_element_type=f32)
            chem_ref[:, at] = (spread_ref[:, at] + time_step * gain) / (
                1.0 + time_step * loss / chem_ref[:, at]
            )
    for j, at in enumerate(folds(species)):
        moved = pick(choice_ref[...], chem_ref[:, at])
        out[0][:, j * CAP : (j + 1) * CAP, :] = moved.reshape(-1, CAP, moved.shape[1])
    left.append(leave(out[0], send_hbm, out_sems.at[0]))
    finish(left)


def stay_kernel(me_ref, rows_ref, place_ref, owner_ref, slot_ref, out_ref, land_ref):
    out_ref[...] = pick(stay_choice(owner_ref[...], slot_ref[...], me_ref[0]), rows_ref[...])
    land_ref[...] = jnp.transpose(landing(place_ref[:, 0:1], rows_ref.shape[0]))


def land_kernel(recv_ref, land_ref, stay_ref, out_hbm, out_sems, *out):
    partners, _, width = recv_ref.shape
    species = out_hbm.shape[1]
    left = []
    for j, at in enumerate(folds(species)):
        got = recv_ref[:, j * CAP : (j + 1) * CAP, :].reshape(partners * CAP, width)
        out[j][...] = pick(land_ref[...], got) + stay_ref[:, at]
        left.append(leave(out[j], out_hbm.at[:, at], out_sems.at[j]))
    finish(left)


def call(kernel, inputs, specs, outputs, scratch=(), limit=6, cost=None):
    outputs = tuple(jax.ShapeDtypeStruct(o, f32) if isinstance(o, tuple) else o for o in outputs)
    return pl.pallas_call(
        kernel,
        out_shape=outputs,
        in_specs=specs,
        out_specs=tuple(VMEM if isinstance(o, jax.ShapeDtypeStruct) else HBM for o in outputs),
        scratch_shapes=list(scratch),
        compiler_params=pltpu.CompilerParams(vmem_limit_bytes=limit * 2**20),
        cost_estimate=cost,
    )(*inputs)


def like(*arrays):
    return [pltpu.VMEM(x.shape, x.dtype) for x in arrays], pltpu.SemaphoreType.DMA((len(arrays),))


def table_cost(species, reactions, tables):
    return pl.CostEstimate(
        flops=40 * species * reactions * tables,
        bytes_accessed=2 * species * reactions * tables,
        transcendentals=0,
    )


def local(
    earlier_kinetics_concentrations,
    thermal_level,
    earlier_fluid_holder,
    earlier_fluid_slot,
    adjacent_volumes,
    interface_spreading_factor,
    species_spreading_coefficient,
    present_kinetics_holder,
    present_kinetics_slot,
    natural_frequency_factor,
    arrhenius_energy,
    consumed_species,
    yielded_species,
):
    n, species = earlier_kinetics_concentrations.shape
    reactions = natural_frequency_factor.shape[0]
    partners = lax.axis_size("cells")
    me = lax.axis_index("cells").astype(i32).reshape(1)
    row = lambda x: x.reshape(1, -1)

    def exchange(x):
        return lax.all_to_all(x, "cells", split_axis=0, concat_axis=0, tiled=True)

    earlier = (
        earlier_kinetics_concentrations,
        row(thermal_level),
        row(earlier_fluid_holder),
        row(earlier_fluid_slot),
    )
    owner, slot = row(present_kinetics_holder), row(present_kinetics_slot)
    pack_scratch, pack_sems = like(*earlier, owner, slot)
    ends = folds(species)
    folded = (partners, CAP * len(ends), species // len(ends))
    (send,) = call(
        pack_kernel,
        (me, *in_hbm(*earlier, owner, slot)),
        [SMEM] + [HBM] * 6,
        ((partners, CAP, species + EXTRA),),
        [*pack_scratch, pack_sems],
    )

    block = largest(reactions, 512, 256, 128)
    product_t, head, done = call(
        product_kernel,
        in_hbm(yielded_species, consumed_species, send),
        [HBM] * 3,
        (
            pltpu.HBM((reactions, species), bf16),
            pltpu.HBM((2 * block, species), bf16),
            (8, 128),
        ),
        [
            pltpu.VMEM((2, reactions), i32),
            pltpu.VMEM((2, 2 * block), i32),
            pltpu.VMEM((reactions, species), bf16),
            pltpu.VMEM((2 * block, species), bf16),
            pltpu.SemaphoreType.DMA((2,)),
            pltpu.SemaphoreType.DMA((reactions // block + 1,)),
        ],
        limit=24,
        cost=table_cost(species, reactions, 1),
    )
    recv = exchange(send)
    ready = (
        owner,
        adjacent_volumes,
        interface_spreading_factor,
        species_spreading_coefficient.reshape(-1, 128),
        natural_frequency_factor.reshape(-1, 128),
        arrhenius_energy.reshape(-1, 128),
    )
    ready_scratch, _ = like(*earlier, *ready)
    state, heat, *prepared, consumed = call(
        prepare_kernel,
        (me, *in_hbm(*earlier, *ready, consumed_species, send)),
        [SMEM] + [HBM] * 12,
        (
            (n, species),
            (n, EXTRA),
            (partners * CAP, n),
            jax.ShapeDtypeStruct((n + 2 * HALO, n), bf16),
            jax.ShapeDtypeStruct((n + 2 * HALO, n), bf16),
            (1, species),
            (n, 128),
            (1, reactions),
            (1, reactions),
            jax.ShapeDtypeStruct((2, reactions), i32),
        ),
        [*ready_scratch, pltpu.SemaphoreType.DMA((11,))],
    )
    flow, heat, to_outer, to_inner, place = call(
        flow_kernel,
        (me, recv, state, heat, done),
        [SMEM] + [VMEM] * 3 + [ANY],
        ((n, species), (n, EXTRA), (HALO, species), (HALO, species), (partners * CAP, EXTRA)),
    )
    inner = [(i, i ^ 1) for i in range(partners)]
    outer = [(i, ((i + 1) ^ 1) - 1) for i in range(1, partners - 1)]
    from_inner = lax.ppermute(to_inner, "cells", inner)
    from_outer = lax.ppermute(to_outer, "cells", outer)
    tables = call(
        react_kernel,
        (consumed, *in_hbm(product_t, head), heat),
        [VMEM, HBM, HBM, ANY],
        (
            jax.ShapeDtypeStruct((species, reactions), bf16),
            jax.ShapeDtypeStruct((reactions, species), bf16),
            jax.ShapeDtypeStruct((reactions, species), bf16),
        ),
        [pltpu.SemaphoreType.DMA((2,))],
        limit=4,
        cost=table_cost(species, reactions, 2),
    )
    spread, chem, send = call(
        chemistry_kernel,
        (me, flow, heat, from_inner, from_outer, *tables, *prepared),
        [SMEM] + [VMEM] * (7 + len(prepared)),
        (
            pltpu.HBM((n, species), f32),
            (n, species),
            pltpu.HBM(folded, f32),
        ),
        [
            pltpu.VMEM((n, reactions), bf16),
            pltpu.VMEM((n, species), bf16),
            pltpu.VMEM((n, species), f32),
            pltpu.SemaphoreType.DMA((2,)),
            pltpu.VMEM(folded, f32),
        ],
        limit=6,
    )
    recv = exchange(send)
    stay, land = call(
        stay_kernel,
        (me, chem, place, owner, slot),
        [SMEM] + [VMEM] * 4,
        ((n, species), (n, partners * CAP)),
    )
    (chem_next,) = call(
        land_kernel,
        (recv, land, stay),
        [VMEM] * 3,
        (pltpu.HBM((n, species), f32),),
        [
            pltpu.SemaphoreType.DMA((len(ends),)),
            *[pltpu.VMEM((n, species // len(ends)), f32) for _ in ends],
        ],
    )
    return (spread, chem_next)


def solution(mesh):
    in_specs = (
        P("cells", None),
        P("cells"),
        P("cells"),
        P("cells"),
        P(None, "cells"),
        P(None, "cells"),
        P(),
        P("cells"),
        P("cells"),
        P(),
        P(),
        P(),
        P(),
    )
    out_specs = (P("cells", None), P("cells", None))
    return jax.shard_map(local, mesh=mesh, in_specs=in_specs, out_specs=out_specs, check_vma=False)
```

```python
import functools

import jax
import jax.numpy as jnp
from jax import lax
from jax.experimental import pallas as pl
from jax.experimental.pallas import tpu as pltpu
from jax.sharding import PartitionSpec as P

NEWTON = 2
HALO = 32
CAP = 2
EXTRA = 128

time_step = 0.5

f32 = jnp.float32
bf16 = jnp.bfloat16
i32 = jnp.int32
i16 = jnp.int16

VMEM = pl.BlockSpec(memory_space=pltpu.VMEM)
SMEM = pl.BlockSpec(memory_space=pltpu.SMEM)
HBM = pl.BlockSpec(memory_space=pltpu.HBM)
ANY = pl.BlockSpec(memory_space=pl.ANY)


def iota(shape, dim):
    return lax.broadcasted_iota(i32, shape, dim)


def largest(total, *wanted):
    return next(b for b in wanted if total % b == 0)


def column(row):
    n = row.shape[1]
    eye = iota((n, n), 0) == iota((n, n), 1)
    return jnp.sum(jnp.where(eye, row, jnp.zeros_like(row)), axis=1, keepdims=True)


def split(x):
    hi = x.astype(bf16)
    return hi, (x - hi.astype(f32)).astype(bf16)


def pick(choice, rows, dims=(((1,), (0,)), ((), ()))):
    choice = choice.astype(bf16)
    hi, mid = split(rows)
    return lax.dot_general(choice, hi, dims, preferred_element_type=f32) + lax.dot_general(
        choice, mid, dims, preferred_element_type=f32
    )


def send_choice(owner, me, partners):
    n = owner.shape[1]
    hits = ((iota((partners, n), 0) == owner) & (owner != me)).astype(f32)
    before = (iota((n, n), 0) < iota((n, n), 1)).astype(bf16)
    earlier = jnp.dot(hits.astype(bf16), before, preferred_element_type=f32)
    within = jnp.sum(earlier * hits, axis=0, keepdims=True).astype(i32)
    position = jnp.where(owner != me, owner * CAP + within, -1)
    return (iota((partners * CAP, n), 0) == position).astype(f32)


def in_hbm(*arrays):
    return tuple(pltpu.with_memory_space_constraint(x, pltpu.HBM) for x in arrays)


def begin(sources, targets, sems):
    copies = [
        pltpu.make_async_copy(source, target, sems.at[i])
        for i, (source, target) in enumerate(zip(sources, targets))
    ]
    for copy in copies:
        copy.start()
    return copies


def pieces(total, *widths):
    width = largest(total, *widths, 256, 128)
    return [slice(first, first + width) for first in range(0, total, width)]


def leave(source, target, sem):
    copy = pltpu.make_async_copy(source, target, sem)
    copy.start()
    return copy


def finish(copies):
    for copy in copies:
        copy.wait()


def beside_rows(values):
    n = values[0].shape[1]
    lane = iota((n, EXTRA), 1)
    out = jnp.zeros((n, EXTRA), f32)
    for i, value in enumerate(values):
        out = jnp.where(lane == i, column(value.astype(f32)), out)
    return out


def flat(ref):
    return jnp.concatenate([ref[q : q + 1, :] for q in range(ref.shape[0])], axis=1)


def landing(places, n):
    return (iota((places.shape[0], n), 1) == places.astype(i32) - 1).astype(f32)


def arrived(recv_ref, places, n):
    partners, cap, width = recv_ref.shape
    got = recv_ref[...].reshape(partners * cap, width)
    return pick(landing(places, n), got, (((0,), (0,)), ((), ())))


def stay_choice(owner, slot, me):
    n = owner.shape[1]
    return ((iota((n, n), 0) == slot) & (owner == me)).astype(f32)


def pack_kernel(
    me_ref,
    rows_hbm,
    temper_hbm,
    owner_hbm,
    slot_hbm,
    next_owner_hbm,
    next_slot_hbm,
    send_ref,
    rows,
    temper,
    owner,
    slot,
    next_owner,
    next_slot,
    sems,
):
    sources = (temper_hbm, owner_hbm, slot_hbm, next_owner_hbm, next_slot_hbm, rows_hbm)
    copies = begin(sources, (temper, owner, slot, next_owner, next_slot, rows), sems)
    finish(copies[:-1])
    partners, cap, _ = send_ref.shape
    species = rows.shape[1]
    choice = send_choice(owner[...], me_ref[0], partners)
    next_choice = send_choice(next_owner[...], me_ref[0], partners)
    none = jnp.zeros_like(temper[...])
    beside = pick(choice, beside_rows((temper[...], slot[...] + 1, none))) + pick(
        next_choice, beside_rows((none, none, next_slot[...] + 1))
    )
    send_ref[:, :, species:] = beside.reshape(partners, cap, EXTRA)
    finish(copies[-1:])
    send_ref[:, :, :species] = pick(choice, rows[...]).reshape(partners, cap, species)


def prepare_kernel(
    me_ref,
    rows_hbm,
    temper_hbm,
    owner_hbm,
    slot_hbm,
    next_owner_hbm,
    adjacent_hbm,
    factor_hbm,
    coefficient_hbm,
    frequency_hbm,
    energy_hbm,
    consumed_hbm,
    after_ref,
    state_ref,
    heat_ref,
    choice_ref,
    weight_hi_ref,
    weight_mid_ref,
    scale_ref,
    total_ref,
    frequency_ref,
    energy_ref,
    consumed_ref,
    rows,
    temper,
    owner,
    slot,
    next_owner,
    adjacent,
    factor,
    coefficient,
    frequency,
    energy,
    sems,
):
    sources = (temper_hbm, owner_hbm, slot_hbm, next_owner_hbm, adjacent_hbm, factor_hbm)
    sources += (coefficient_hbm, frequency_hbm, energy_hbm, consumed_hbm, rows_hbm)
    targets = (temper, owner, slot, next_owner, adjacent, factor)
    targets += (coefficient, frequency, energy, consumed_ref, rows)
    copies = begin(sources, targets, sems)
    finish(copies[:-1])
    me = me_ref[0]
    choice_ref[...] = send_choice(next_owner[...], me, choice_ref.shape[0] // CAP)
    weight, total = face_weights(me, adjacent[...], factor[...])
    weight_hi_ref[...], weight_mid_ref[...] = split(weight)
    scale_ref[...] = time_step * flat(coefficient)
    total_ref[...] = jnp.broadcast_to(column(total), total_ref.shape)
    frequency_ref[...] = flat(frequency)
    energy_ref[...] = flat(energy)
    stay = stay_choice(owner[...], slot[...], me)
    heat_ref[...] = pick(stay, jnp.broadcast_to(column(temper[...]), heat_ref.shape))
    finish(copies[-1:])
    state_ref[...] = pick(stay, rows[...])


def flow_kernel(
    me_ref,
    recv_ref,
    state_ref,
    temper_ref,
    after_ref,
    flow_ref,
    heat_ref,
    outer_ref,
    inner_ref,
    place_ref,
):
    n, species = state_ref.shape
    partners, cap, width = recv_ref.shape
    beside = recv_ref[:, :, species:].reshape(partners * cap, EXTRA)
    rows = arrived(recv_ref, beside[:, 1:2], n)
    state = rows[:, :species] + state_ref[...]
    flow_ref[...] = state
    heat_ref[...] = rows[:, species:] + temper_ref[...]
    place_ref[...] = jnp.broadcast_to(beside[:, 2:3], place_ref.shape)
    even = lax.rem(me_ref[0], 2) == 0
    inner_ref[...] = jnp.where(even, state[n - HALO :], state[:HALO])
    outer_ref[...] = jnp.where(even, state[:HALO], state[n - HALO :])


def face_weights(me, adjacent, factor):
    n = adjacent.shape[1]
    index = adjacent - me * n + HALO
    rows = iota((n + 2 * HALO, n), 0)
    weight = jnp.zeros((n + 2 * HALO, n), f32)
    total = jnp.zeros((1, n), f32)
    for face in range(adjacent.shape[0]):
        weight += jnp.where(rows == index[face : face + 1], factor[face : face + 1], 0.0)
        total += factor[face : face + 1]
    return weight, total


def table(index_iota, first, second):
    one, zero = jnp.ones((), bf16), jnp.zeros((), bf16)
    return jnp.where(index_iota == first, one, zero) + jnp.where(index_iota == second, one, zero)


def column_table(pairs):
    block = pairs.shape[1]
    columns = jnp.transpose(
        jnp.concatenate([pairs, jnp.zeros((6, block), i32)], axis=0)
    ).astype(i16)

    def rows(species):
        return table(
            iota((block, species), 1).astype(i16), columns[:, 0:1], columns[:, 1:2]
        )

    return rows


def product_kernel(
    yielded_hbm,
    consumed_hbm,
    after_hbm,
    product_t_hbm,
    head_hbm,
    done_ref,
    yielded,
    consumed,
    product_t,
    head,
    sems,
    out_sems,
):
    reactions, species = product_t.shape
    block = largest(reactions, 512, 256, 128)
    blocks = reactions // block
    many = head.shape[0]
    finish(begin((yielded_hbm, consumed_hbm.at[:, :many]), (yielded, consumed), sems))

    def out(b):
        at = pl.ds(pl.multiple_of(b * block, block), block)
        return pltpu.make_async_copy(
            product_t.at[at, :], product_t_hbm.at[at, :], out_sems.at[b]
        )

    def fill(b, carry):
        at = pl.ds(pl.multiple_of(b * block, block), block)
        product_t[at, :] = column_table(yielded[:, at])(species)
        out(b).start()
        return carry

    def drain(b, carry):
        out(b).wait()
        return carry

    lax.fori_loop(0, blocks, fill, 0, unroll=largest(blocks, 3, 2, 1))
    for first in range(0, many, block):
        at = slice(first, first + block)
        head[at, :] = column_table(consumed[:, at])(species)
    left = leave(head, head_hbm, out_sems.at[blocks])
    done_ref[...] = jnp.zeros_like(done_ref)
    lax.fori_loop(0, blocks, drain, 0)
    left.wait()


def react_kernel(
    consumed_ref,
    product_t_hbm,
    head_hbm,
    after_ref,
    react_ref,
    react_t_ref,
    product_t_ref,
    sems,
):
    many = head_hbm.shape[0]
    targets = (product_t_ref, react_t_ref.at[:many, :])
    copies = begin((product_t_hbm, head_hbm), targets, sems)
    species, reactions = react_ref.shape
    block = largest(reactions, 512, 256, 128)
    down_species = iota((species, block), 0).astype(i16)

    def fill(b, carry):
        at = pl.ds(pl.multiple_of(b * block, block), block)
        used = consumed_ref[:, at]
        react_ref[:, at] = table(down_species, used[0:1].astype(i16), used[1:2].astype(i16))
        return carry

    def fill_t(b, carry):
        at = pl.ds(pl.multiple_of(b * block, block), block)
        react_t_ref[at, :] = column_table(consumed_ref[:, at])(species)
        return carry

    lax.fori_loop(0, reactions // block, fill, 0)
    blocks = reactions // block
    odd = many // block + (blocks - many // block) % 3
    lax.fori_loop(many // block, odd, fill_t, 0)
    lax.fori_loop(odd, blocks, fill_t, 0, unroll=3)
    finish(copies)


def chemistry_kernel(
    me_ref,
    flow_ref,
    heat_ref,
    inner_ref,
    outer_ref,
    react_ref,
    react_t_ref,
    product_t_ref,
    choice_ref,
    weight_hi_ref,
    weight_mid_ref,
    scale_ref,
    total_ref,
    frequency_ref,
    energy_ref,
    spread_hbm,
    chem_ref,
    send_hbm,
    rate_ref,
    log_ref,
    spread_ref,
    out_sems,
    *out,
):
    flow = flow_ref[...]
    even = lax.rem(me_ref[0], 2) == 0
    inner, outer = inner_ref[...], outer_ref[...]
    extended = jnp.concatenate(
        [jnp.where(even, outer, inner), flow, jnp.where(even, inner, outer)], axis=0
    )
    e_hi, e_mid = split(extended)
    dims = (((0,), (0,)), ((), ()))
    coupling = (
        lax.dot_general(weight_hi_ref[...], e_hi, dims, preferred_element_type=f32)
        + lax.dot_general(weight_hi_ref[...], e_mid, dims, preferred_element_type=f32)
        + lax.dot_general(weight_mid_ref[...], e_hi, dims, preferred_element_type=f32)
    )
    scale = scale_ref[...]
    spread = (flow + scale * coupling) / (1.0 + scale * total_ref[:, 0:1])
    spread_ref[...] = spread
    left = [leave(spread_ref, spread_hbm, out_sems.at[len(out)])]
    chem_ref[...] = spread
    inverse = 1.0 / heat_ref[:, 0:1]
    species, reactions = react_ref.shape
    across = largest(reactions, 512, 256, 128)
    down = largest(species, 256, 128)
    tiles = [slice(first, first + down) for first in range(0, species, down)]

    for turn in range(NEWTON):
        log_ref[...] = jnp.log(chem_ref[...]).astype(bf16)
        for first in range(0, reactions, across):
            at = slice(first, first + across)
            exponent = jnp.dot(log_ref[...], react_ref[:, at], preferred_element_type=f32)
            log_rate = frequency_ref[:, at] - energy_ref[:, at] * inverse
            rate_ref[:, at] = jnp.exp(log_rate + exponent).astype(bf16)
        for at in tiles:
            loss = jnp.dot(rate_ref[...], react_t_ref[:, at], preferred_element_type=f32)
            gain = jnp.dot(rate_ref[...], product_t_ref[:, at], preferred_element_type=f32)
            chem_ref[:, at] = (spread_ref[:, at] + time_step * gain) / (
                1.0 + time_step * loss / chem_ref[:, at]
            )
    for i, at in enumerate(pieces(species, 768, 512)):
        out[i][...] = pick(choice_ref[...], chem_ref[:, at]).reshape(out[i].shape)
        left.append(leave(out[i], send_hbm.at[:, :, at], out_sems.at[i]))
    finish(left)


def stay_kernel(me_ref, rows_ref, place_ref, owner_ref, slot_ref, out_ref, land_ref):
    out_ref[...] = pick(stay_choice(owner_ref[...], slot_ref[...], me_ref[0]), rows_ref[...])
    land_ref[...] = jnp.transpose(landing(place_ref[:, 0:1], rows_ref.shape[0]))


def land_kernel(recv_ref, land_ref, stay_ref, out_hbm, out_sems, *out):
    partners, cap, species = recv_ref.shape
    left = []
    for i, at in enumerate(pieces(species, 384)):
        got = recv_ref[:, :, at].reshape(partners * cap, -1)
        out[i][...] = pick(land_ref[...], got) + stay_ref[:, at]
        left.append(leave(out[i], out_hbm.at[:, at], out_sems.at[i]))
    finish(left)


def call(kernel, inputs, specs, outputs, scratch=(), limit=6, cost=None):
    outputs = tuple(jax.ShapeDtypeStruct(o, f32) if isinstance(o, tuple) else o for o in outputs)
    return pl.pallas_call(
        kernel,
        out_shape=outputs,
        in_specs=specs,
        out_specs=tuple(VMEM if isinstance(o, jax.ShapeDtypeStruct) else HBM for o in outputs),
        scratch_shapes=list(scratch),
        compiler_params=pltpu.CompilerParams(vmem_limit_bytes=limit * 2**20),
        cost_estimate=cost,
    )(*inputs)


def like(*arrays):
    return [pltpu.VMEM(x.shape, x.dtype) for x in arrays], pltpu.SemaphoreType.DMA((len(arrays),))


def table_cost(species, reactions, tables):
    return pl.CostEstimate(
        flops=40 * species * reactions * tables,
        bytes_accessed=2 * species * reactions * tables,
        transcendentals=0,
    )


def local(
    earlier_kinetics_concentrations,
    thermal_level,
    earlier_fluid_holder,
    earlier_fluid_slot,
    adjacent_volumes,
    interface_spreading_factor,
    species_spreading_coefficient,
    present_kinetics_holder,
    present_kinetics_slot,
    natural_frequency_factor,
    arrhenius_energy,
    consumed_species,
    yielded_species,
):
    n, species = earlier_kinetics_concentrations.shape
    reactions = natural_frequency_factor.shape[0]
    partners = lax.axis_size("cells")
    me = lax.axis_index("cells").astype(i32).reshape(1)
    row = lambda x: x.reshape(1, -1)

    def exchange(x):
        return lax.all_to_all(x, "cells", split_axis=0, concat_axis=0, tiled=True)

    earlier = (
        earlier_kinetics_concentrations,
        row(thermal_level),
        row(earlier_fluid_holder),
        row(earlier_fluid_slot),
    )
    owner, slot = row(present_kinetics_holder), row(present_kinetics_slot)
    pack_scratch, pack_sems = like(*earlier, owner, slot)
    parts = pieces(species, 768, 512)
    parts_scratch = [pltpu.VMEM((partners, CAP, species // len(parts)), f32) for _ in parts]
    (send,) = call(
        pack_kernel,
        (me, *in_hbm(*earlier, owner, slot)),
        [SMEM] + [HBM] * 6,
        ((partners, CAP, species + EXTRA),),
        [*pack_scratch, pack_sems],
    )

    block = largest(reactions, 512, 256, 128)
    product_t, head, done = call(
        product_kernel,
        in_hbm(yielded_species, consumed_species, send),
        [HBM] * 3,
        (
            pltpu.HBM((reactions, species), bf16),
            pltpu.HBM((2 * block, species), bf16),
            (8, 128),
        ),
        [
            pltpu.VMEM((2, reactions), i32),
            pltpu.VMEM((2, 2 * block), i32),
            pltpu.VMEM((reactions, species), bf16),
            pltpu.VMEM((2 * block, species), bf16),
            pltpu.SemaphoreType.DMA((2,)),
            pltpu.SemaphoreType.DMA((reactions // block + 1,)),
        ],
        limit=24,
        cost=table_cost(species, reactions, 1),
    )
    recv = exchange(send)
    ready = (
        owner,
        adjacent_volumes,
        interface_spreading_factor,
        species_spreading_coefficient.reshape(-1, 128),
        natural_frequency_factor.reshape(-1, 128),
        arrhenius_energy.reshape(-1, 128),
    )
    ready_scratch, _ = like(*earlier, *ready)
    state, heat, *prepared, consumed = call(
        prepare_kernel,
        (me, *in_hbm(*earlier, *ready, consumed_species, send)),
        [SMEM] + [HBM] * 12,
        (
            (n, species),
            (n, EXTRA),
            (partners * CAP, n),
            jax.ShapeDtypeStruct((n + 2 * HALO, n), bf16),
            jax.ShapeDtypeStruct((n + 2 * HALO, n), bf16),
            (1, species),
            (n, 128),
            (1, reactions),
            (1, reactions),
            jax.ShapeDtypeStruct((2, reactions), i32),
        ),
        [*ready_scratch, pltpu.SemaphoreType.DMA((11,))],
    )
    flow, heat, to_outer, to_inner, place = call(
        flow_kernel,
        (me, recv, state, heat, done),
        [SMEM] + [VMEM] * 3 + [ANY],
        ((n, species), (n, EXTRA), (HALO, species), (HALO, species), (partners * CAP, EXTRA)),
    )
    inner = [(i, i ^ 1) for i in range(partners)]
    outer = [(i, ((i + 1) ^ 1) - 1) for i in range(1, partners - 1)]
    from_inner = lax.ppermute(to_inner, "cells", inner)
    from_outer = lax.ppermute(to_outer, "cells", outer)
    tables = call(
        react_kernel,
        (consumed, *in_hbm(product_t, head), heat),
        [VMEM, HBM, HBM, ANY],
        (
            jax.ShapeDtypeStruct((species, reactions), bf16),
            jax.ShapeDtypeStruct((reactions, species), bf16),
            jax.ShapeDtypeStruct((reactions, species), bf16),
        ),
        [pltpu.SemaphoreType.DMA((2,))],
        limit=4,
        cost=table_cost(species, reactions, 2),
    )
    spread, chem, send = call(
        chemistry_kernel,
        (me, flow, heat, from_inner, from_outer, *tables, *prepared),
        [SMEM] + [VMEM] * (7 + len(prepared)),
        (
            pltpu.HBM((n, species), f32),
            (n, species),
            pltpu.HBM((partners, CAP, species), f32),
        ),
        [
            pltpu.VMEM((n, reactions), bf16),
            pltpu.VMEM((n, species), bf16),
            pltpu.VMEM((n, species), f32),
            pltpu.SemaphoreType.DMA((len(parts) + 1,)),
            *parts_scratch,
        ],
        limit=6,
    )
    recv = exchange(send)
    stay, land = call(
        stay_kernel,
        (me, chem, place, owner, slot),
        [SMEM] + [VMEM] * 4,
        ((n, species), (n, partners * CAP)),
    )
    ends = pieces(species, 384)
    (chem_next,) = call(
        land_kernel,
        (recv, land, stay),
        [VMEM] * 3,
        (pltpu.HBM((n, species), f32),),
        [
            pltpu.SemaphoreType.DMA((len(ends),)),
            *[pltpu.VMEM((n, species // len(ends)), f32) for _ in ends],
        ],
    )
    return (spread, chem_next)


def solution(mesh):
    in_specs = (
        P("cells", None),
        P("cells"),
        P("cells"),
        P("cells"),
        P(None, "cells"),
        P(None, "cells"),
        P(),
        P("cells"),
        P("cells"),
        P(),
        P(),
        P(),
        P(),
    )
    out_specs = (P("cells", None), P("cells", None))
    return jax.shard_map(local, mesh=mesh, in_specs=in_specs, out_specs=out_specs, check_vma=False)
```
